512 devices in a mesh: scene: 4 (over x), dir: 2 (over z_hi), tile: 64 (over z_lo, y, core).
Axes of the slice: x: 4, y: 8, z: 8 (z_hi: 2, z_lo: 4; z = z_hi * 4 + z_lo), core: 2. Of those that a mesh axis runs over, the one named last changes fastest.
Arguments:
- tiles: bfloat16 [256, 16, 16, 384], P(('scene', 'tile')), parts along dimension 0, may hold values from -6 to 6
- cotangent: bfloat16 [256, 16, 16, 384], P(('scene', 'tile')), parts along dimension 0, may hold values from -6 to 6
- xproj_w: bfloat16 [2, 2, 384, 44], P('dir'), may hold values from -0.3125 to 0.3125
- dtproj_w: bfloat16 [2, 2, 12, 384], P('dir'), may hold values from -1.75 to 1.75
- dt_bias: float32 [2, 2, 384], P('dir'), may hold values from -6 to -4
- a_log: float32 [2, 2, 16, 384], P('dir'), as said below
- skip_d: float32 [2, 2, 384], P('dir'), may hold values from 0.5 to 1.5
Outputs:
- y_out: bfloat16 [256, 16, 16, 384], P(('scene', 'tile')), parts along dimension 0
- du_out: bfloat16 [256, 16, 16, 384], P(('scene', 'tile')), parts along dimension 0
- d_xproj: float32 [8, 2, 384, 44], P(('scene', 'dir')), parts along dimension 0
The draws below stay inside these ranges and needn't reach their ends.
There are 4 independent parts, one for each index of `scene`. The reference program is written for one: setup_inputs(seed, part) draws one part's arguments, and reference() takes and returns one part's arrays. A program takes and returns all parts, laid end to end along the dimension named above; an argument that names none is the same for every part. Nothing has to cross between parts.
Inputs may be any that keep to these rules, and one draw needn't show every extreme that they name: `a_log`: every entry lies between log(0.5 / 16384) and log(15).
All inputs are finite; a program needn't handle non-finite values.
Results may differ from the reference program's by a relative error of at most 0.0025.
Values may be sent and summed in bfloat16 or wider, within the bound.
A program may use at most 128 MiB of HBM per device.

```python
import math
import jax
import jax.numpy as jnp
from jax import lax

E = 384
NSTATE = 16
RANK = 12
TS = 16
TILES = 64
SIDE = 128


def draw_a_log(key, part):
    key = jax.random.fold_in(key, 11)
    length = float(SIDE * SIDE)
    low_end = math.log(0.5 / length)
    high_end = math.log(15.0)
    return jax.random.uniform(key, (2, 2, NSTATE, E), jnp.float32, low_end, high_end)


def block_levels(stream_key, extent, pieces, low, largest):
    def one(axis_at, blocks):
        heights = jax.random.uniform(jax.random.fold_in(jax.random.fold_in(stream_key, 6), axis_at), (blocks,), jnp.float32, low / len(pieces), largest / len(pieces))
        return jnp.repeat(jnp.exp(heights), extent[axis_at] // blocks).reshape((-1,) + (1,) * (len(extent) - axis_at - 1))

    gain = one(*pieces[0])
    for cut in pieces[1:]:
        gain = gain * one(*cut)
    return gain


def scatter_about(stream_key, dims, deviation, bound, split=(), held_as=jnp.bfloat16):
    entries = deviation * jax.random.normal(stream_key, dims, jnp.float32)
    if split:
        entries = entries * block_levels(stream_key, dims, split, -0.22, 0.18)
    return jnp.clip(entries, -bound, bound).astype(held_as)


def setup_inputs(seed: int = 0, part: int = 0) -> dict:
    key_of = jax.random.split(jax.random.key(seed), 8)
    part_splits = jax.random.split(jax.random.fold_in(key_of[7], part), 8)
    tiles = scatter_about(part_splits[0], (TILES, TS, TS, E), 1.0, 6.0, ((0, 64),))
    cotangent = scatter_about(part_splits[1], (TILES, TS, TS, E), 1.0, 6.0, ((0, 64),))
    xproj_w = scatter_about(key_of[2], (2, 2, E, RANK + 2 * NSTATE), E ** -0.5, 0.3125, ((0, 2),))
    dtproj_w = scatter_about(key_of[3], (2, 2, RANK, E), RANK ** -0.5, 1.75, ((0, 2),))
    dt_bias = jnp.clip(-6.0 + 2.0 * jax.random.uniform(key_of[4], (2, 2, E), jnp.float32) ** block_levels(key_of[4], (2, 2, E), ((0, 2),), -0.2, 0.2), -6.0, -4.0)
    a_log = draw_a_log(jax.random.fold_in(key_of[7], 71), part)
    skip_d = jnp.clip(0.5 + 1.0 * jax.random.uniform(key_of[6], (2, 2, E), jnp.float32) ** block_levels(key_of[6], (2, 2, E), ((0, 2),), -0.2, 0.2), 0.5, 1.5)
    return {"tiles": tiles, "cotangent": cotangent, "xproj_w": xproj_w, "dtproj_w": dtproj_w, "dt_bias": dt_bias, "a_log": a_log, "skip_d": skip_d}


highest = lax.Precision.HIGHEST

def project(values, mixing, step_proj, step_bias):
    low_rank = step_proj.shape[0]
    states = (mixing.shape[1] - low_rank) // 2
    mixed = jnp.dot(values, mixing, precision=highest)
    step_sizes = jax.nn.softplus(jnp.dot(mixed[:, :low_rank], step_proj, precision=highest) + step_bias)
    return (step_sizes, mixed[:, low_rank:low_rank + states], mixed[:, low_rank + states:])

def scan_sequence(values, step_sizes, inject, read_cols, decay_rates, skip_gain):
    length = values.shape[0]
    block_len = math.gcd(length, 128)
    blocks = length // block_len

    def advance_token(carry_state, token):
        value_row, size_row, inject_row, read_row = token
        carry_state = jnp.exp(size_row[None, :] * decay_rates) * carry_state + (size_row * value_row)[None, :] * inject_row[:, None]
        return (carry_state, lax.optimization_barrier(jnp.sum(carry_state * read_row[:, None], axis=0)) + skip_gain * value_row)

    def advance_block(carry_state, block_data):
        return lax.scan(advance_token, carry_state, block_data)
    members = tuple((member.reshape(blocks, block_len, member.shape[1]) for member in (values, step_sizes, inject, read_cols)))
    start_state = jnp.zeros(decay_rates.shape, jnp.float32)
    unused, outputs = lax.scan(jax.checkpoint(advance_block), start_state, members)
    return outputs.reshape(length, values.shape[1])

def scene_field(scene_image, mixing_all, proj_all, bias_all, log_rates, skip_all):
    side = scene_image.shape[0]
    channels = scene_image.shape[2]
    field = jnp.zeros(scene_image.shape, jnp.float32)
    for direction in range(2):
        for axis_no in range(2):
            oriented = scene_image if axis_no == 0 else jnp.transpose(scene_image, (1, 0, 2))
            sequence = oriented.reshape(side * side, channels)
            if direction == 1:
                sequence = sequence[::-1]
            step_sizes, inject, read_cols = project(sequence, mixing_all[direction, axis_no], proj_all[direction, axis_no], bias_all[direction, axis_no])
            outputs = scan_sequence(sequence, step_sizes, inject, read_cols, -jnp.exp(log_rates[direction, axis_no]), skip_all[direction, axis_no])
            if direction == 1:
                outputs = outputs[::-1]
            outputs = outputs.reshape(side, side, channels)
            if axis_no == 1:
                outputs = jnp.transpose(outputs, (1, 0, 2))
            field = field + outputs
    return field

def to_image(tile_data, grid_side):
    tile_side = tile_data.shape[1]
    channels = tile_data.shape[3]
    arranged = tile_data.reshape(grid_side, grid_side, tile_side, tile_side, channels).transpose(0, 2, 1, 3, 4)
    return arranged.reshape(grid_side * tile_side, grid_side * tile_side, channels)

def to_tiles(image_data, grid_side):
    tile_side = image_data.shape[0] // grid_side
    channels = image_data.shape[2]
    arranged = image_data.reshape(grid_side, tile_side, grid_side, tile_side, channels).transpose(0, 2, 1, 3, 4)
    return arranged.reshape(grid_side * grid_side, tile_side, tile_side, channels)

def reference(tiles, cotangent, xproj_w, dtproj_w, dt_bias, a_log, skip_d):
    grid_side = math.isqrt(tiles.shape[0])
    scene_image = to_image(tiles.astype(jnp.float32), grid_side)
    cot_image = to_image(cotangent.astype(jnp.float32), grid_side)
    proj_all = dtproj_w.astype(jnp.float32)

    def forward(image_data, mixing_all):
        return scene_field(image_data, mixing_all, proj_all, dt_bias, a_log, skip_d)
    field, back = jax.vjp(forward, scene_image, xproj_w.astype(jnp.float32))
    image_grad, mixing_grad = back(cot_image)
    return (to_tiles(field, grid_side).astype(jnp.bfloat16), to_tiles(image_grad, grid_side).astype(jnp.bfloat16), mixing_grad)
```

```python
import jax
import jax.numpy as jnp
from jax import lax
from jax.experimental import pallas as pl
from jax.experimental.pallas import tpu as pltpu
from jax.sharding import PartitionSpec as P

MESH = pl.DeviceIdType.MESH

E = 384
NS = 16
TS = 16
TOK = 256
LOG2E = 1.4426950408889634
LN2 = 0.6931471805599453
NT = (((1,), (1,)), ((), ()))
TN = (((0,), (0,)), ((), ()))
NN = (((1,), (0,)), ((), ()))


def dot(lhs, rhs, dims=NN):
    return lax.dot_general(lhs, rhs, dims, preferred_element_type=jnp.float32)


def halves(vals):
    top = vals.astype(jnp.bfloat16)
    return top, (vals - top.astype(jnp.float32)).astype(jnp.bfloat16)


def thirds(vals):
    top = vals.astype(jnp.bfloat16)
    rest = vals - top.astype(jnp.float32)
    return (top,) + halves(rest)


def swap_matrix():
    row = lax.broadcasted_iota(jnp.int32, (TOK, TOK), 0)
    col = lax.broadcasted_iota(jnp.int32, (TOK, TOK), 1)
    return ((row % TS) * TS + row // TS == col).astype(jnp.bfloat16)


def prepare(axis, x_ref, cot_ref, xw_ref, dw_ref, bias_ref, alog_ref, u_sc, cot_sc, dt_sc, w_sc, bc_sc, rate_sc):
    if axis == 0:
        swap = swap_matrix()
        xs = dot(swap, x_ref[...])
        cs = dot(swap, cot_ref[...])
        xb = xs.astype(jnp.bfloat16)
    else:
        xb = x_ref[...]
        xs = xb.astype(jnp.float32)
        cs = cot_ref[...].astype(jnp.float32)
    u_sc[...] = xs
    cot_sc[...] = cs
    mixed = dot(xb, xw_ref[axis])
    for n in range(2 * NS):
        bc_sc[:, n * 128 : (n + 1) * 128] = jnp.broadcast_to(mixed[:, 12 + n : 13 + n], (TOK, 128))
    proj = dw_ref[axis]
    raw = sum(dot(part, proj) for part in thirds(mixed))
    raw = raw + bias_ref[axis : axis + 1, :]
    dt = jnp.maximum(raw, 0.0) + jnp.log1p(jnp.exp(-jnp.abs(raw)))
    dt_sc[...] = dt
    w_sc[...] = dt * xs
    rate_sc[...] = -LOG2E * jnp.exp(alog_ref[axis])
    return xb


def maps_kernel(rev_ref, x_ref, cot_ref, xw_ref, dw_ref, bias_ref, alog_ref, m_ref, u_sc, cot_sc, dt_sc, w_sc, bc_sc, rate_sc):
    rev = rev_ref[0]
    for axis in range(2):
        prepare(axis, x_ref, cot_ref, xw_ref, dw_ref, bias_ref, alog_ref, u_sc, cot_sc, dt_sc, w_sc, bc_sc, rate_sc)
        size = dt_sc[0:TS, :]
        for p in range(1, TS):
            size = size + dt_sc[p * TS : (p + 1) * TS, :]
        for j in range(8):
            m_ref[axis, j, 4] = size

        def unit(lh, carry, axis=axis):
            line0 = pl.multiple_of(lh * 8, 8)
            for et in range(3):
                lanes = slice(et * 128, (et + 1) * 128)
                for half in range(2):
                    ns = range(half * 8, half * 8 + 8)
                    rates = [jnp.broadcast_to(rate_sc[n : n + 1, lanes], (8, 128)) for n in ns]

                    def step(t, state):
                        hs, qs, gs = state
                        p = rev * 15 + (1 - 2 * rev) * t
                        rows = pl.ds(pl.multiple_of(p * TS + line0, 8), 8)
                        dt = dt_sc[rows, lanes]
                        w = w_sc[rows, lanes]
                        ct = cot_sc[rows, lanes]
                        nh, nq, ng = [], [], []
                        for m, n in enumerate(ns):
                            a = jnp.exp2(dt * rates[m])
                            b = bc_sc[rows, n * 128 : (n + 1) * 128]
                            c = bc_sc[rows, (NS + n) * 128 : (NS + n + 1) * 128]
                            nh.append(a * hs[m] + w * b)
                            q = a * qs[m]
                            nq.append(q)
                            ng.append(gs[m] + q * (c * ct))
                        return nh, nq, ng

                    zero = [jnp.zeros((8, 128), jnp.float32)] * 8
                    one = [jnp.ones((8, 128), jnp.float32)] * 8
                    hs, qs, gs = lax.fori_loop(0, TS, step, (zero, one, zero))
                    for m, n in enumerate(ns):
                        m_ref[axis, n // 2, n % 2, pl.ds(line0, 8), lanes] = hs[m]
                        m_ref[axis, n // 2, 2 + n % 2, pl.ds(line0, 8), lanes] = gs[m]
            return carry

        lax.fori_loop(0, 2, unit, 0)


def finish_kernel(rev_ref, x_ref, cot_ref, xw_ref, dw_ref, bias_ref, alog_ref, skip_ref, r_ref,
                  y_ref, du_ref, dx_ref,
                  u_sc, cot_sc, dt_sc, w_sc, bc_sc, rate_sc, dbc_sc, ah_sc, y_sc, du_sc, ddt_sc):
    rev = rev_ref[0]
    for axis in range(2):
        xb = prepare(axis, x_ref, cot_ref, xw_ref, dw_ref, bias_ref, alog_ref, u_sc, cot_sc, dt_sc, w_sc, bc_sc, rate_sc)

        def unit(lh, carry, axis=axis):
            line0 = pl.multiple_of(lh * 8, 8)
            lines = pl.ds(line0, 8)
            for et in range(3):
                lanes = slice(et * 128, (et + 1) * 128)
                rates = [jnp.broadcast_to(rate_sc[n : n + 1, lanes], (8, 128)) for n in range(NS)]
                skip = jnp.broadcast_to(skip_ref[axis : axis + 1, lanes], (8, 128))

                def forward(t, hs):
                    p = rev * 15 + (1 - 2 * rev) * t
                    rows = pl.ds(pl.multiple_of(p * TS + line0, 8), 8)
                    dt = dt_sc[rows, lanes]
                    w = w_sc[rows, lanes]
                    ct = cot_sc[rows, lanes]
                    y = skip * u_sc[rows, lanes]
                    out = []
                    for n in range(NS):
                        a = jnp.exp2(dt * rates[n])
                        ah = a * hs[n]
                        ah_sc[t, n] = ah
                        h = ah + w * bc_sc[rows, n * 128 : (n + 1) * 128]
                        cols = slice((NS + n) * 128, (NS + n + 1) * 128)
                        y = y + h * bc_sc[rows, cols]
                        dc = h * ct
                        if et > 0:
                            dc = dc + dbc_sc[rows, cols]
                        dbc_sc[rows, cols] = dc
                        out.append(h)
                    y_sc[et, rows, :] = y
                    return out

                lax.fori_loop(0, TS, forward, [r_ref[axis, n // 2, n % 2, lines, lanes] for n in range(NS)])

                def backward(i, gs):
                    t = 15 - i
                    p = rev * 15 + (1 - 2 * rev) * t
                    rows = pl.ds(pl.multiple_of(p * TS + line0, 8), 8)
                    dt = dt_sc[rows, lanes]
                    w = w_sc[rows, lanes]
                    ct = cot_sc[rows, lanes]
                    dw = jnp.zeros((8, 128), jnp.float32)
                    dr = jnp.zeros((8, 128), jnp.float32)
                    out = []
                    for n in range(NS):
                        a = jnp.exp2(dt * rates[n])
                        g = gs[n] + bc_sc[rows, (NS + n) * 128 : (NS + n + 1) * 128] * ct
                        cols = slice(n * 128, (n + 1) * 128)
                        db = g * w
                        if et > 0:
                            db = db + dbc_sc[rows, cols]
                        dbc_sc[rows, cols] = db
                        dw = dw + g * bc_sc[rows, cols]
                        dr = dr + (g * ah_sc[t, n]) * rates[n]
                        out.append(a * g)
                    ddt_sc[rows, lanes] = dr * LN2 + dw * u_sc[rows, lanes]
                    du_sc[et, rows, :] = dw * dt + skip * ct
                    return out

                lax.fori_loop(0, TS, backward, [r_ref[axis, n // 2, 2 + n % 2, lines, lanes] for n in range(NS)])
            return carry

        lax.fori_loop(0, 2, unit, 0)
        dt = dt_sc[...]
        small = dt * (1.0 - dt * (0.5 - dt * (1.0 / 6.0 - dt * (1.0 / 24.0))))
        dv = ddt_sc[...] * jnp.where(dt < 0.03, small, 1.0 - jnp.exp(-dt))
        proj = dw_ref[axis]
        dmix = sum(dot(part, proj, NT) for part in halves(dv))
        row = lax.broadcasted_iota(jnp.int32, (512, 128), 0)
        col = lax.broadcasted_iota(jnp.int32, (512, 128), 1)
        for blk in range(8):
            pick = (col == 12 + blk * 4 + row // 128).astype(jnp.bfloat16)
            for part in halves(dbc_sc[:, blk * 512 : (blk + 1) * 512]):
                dmix = dmix + dot(part, pick)
        parts = halves(dmix)
        weight = xw_ref[axis]
        dx_ref[axis] = sum(dot(part, xb, TN) for part in parts)[: dx_ref.shape[1]]
        through = sum(dot(part, weight, NT) for part in parts)
        for et in range(3):
            lanes = slice(et * 128, (et + 1) * 128)
            if axis == 0:
                du_sc[et] = du_sc[et] + through[:, lanes]
                for i in range(TS):
                    rows = slice(i * TS, (i + 1) * TS)
                    y_ref[rows, lanes] = y_sc[et, pl.ds(i, TS, stride=TS), :]
                    du_ref[rows, lanes] = du_sc[et, pl.ds(i, TS, stride=TS), :]
            else:
                y_ref[:, lanes] = y_ref[:, lanes] + y_sc[et]
                du_ref[:, lanes] = du_ref[:, lanes] + du_sc[et] + through[:, lanes]


def f32(*shape):
    return jax.ShapeDtypeStruct(shape, jnp.float32)


PREP = [pltpu.VMEM((TOK, E), jnp.float32)] * 4 + [pltpu.VMEM((TOK, 4096), jnp.float32), pltpu.VMEM((NS, E), jnp.float32)]
SMEM = pl.BlockSpec(memory_space=pltpu.SMEM)
VMEM = pl.BlockSpec(memory_space=pltpu.VMEM)


def line_maps(rev, x, cot, xw, dw, bias, alog):
    return pl.pallas_call(
        maps_kernel,
        out_shape=f32(2, 8, 5, TS, E),
        in_specs=[SMEM] + [VMEM] * 6,
        out_specs=VMEM,
        scratch_shapes=PREP,
        compiler_params=pltpu.CompilerParams(vmem_limit_bytes=48 * 2**20),
        name="line_maps",
    )(rev, x, cot, xw, dw, bias, alog)


def finish(rev, x, cot, xw, dw, bias, alog, skip, carries):
    return pl.pallas_call(
        finish_kernel,
        out_shape=(f32(TOK, E), f32(TOK, E), f32(2, 64, E)),
        in_specs=[SMEM] + [VMEM] * 8,
        out_specs=(VMEM, VMEM, VMEM),
        scratch_shapes=PREP + [pltpu.VMEM((TOK, 4096), jnp.float32), pltpu.VMEM((TS, NS, 8, 128), jnp.float32)]
        + [pltpu.VMEM((3, TOK, 128), jnp.float32)] * 2
        + [pltpu.VMEM((TOK, E), jnp.float32)],
        compiler_params=pltpu.CompilerParams(vmem_limit_bytes=48 * 2**20),
        name="finish",
    )(rev, x, cot, xw, dw, bias, alog, skip, carries)


def tile_peers(tile):
    row, col = tile // 8, tile % 8
    along_row = [row * 8 + lax.rem(col + d, 8) for d in range(1, 8)]
    along_col = [lax.rem(row + d, 8) * 8 + col for d in range(1, 8)]
    return along_row, along_col


def greet(peers, partner=None):
    barrier = pltpu.get_barrier_semaphore()
    for peer in peers:
        pl.semaphore_signal(barrier, inc=1, device_id={"tile": peer}, device_id_type=MESH)
    count = len(peers)
    if partner is not None:
        pl.semaphore_signal(barrier, inc=1, device_id={"dir": partner}, device_id_type=MESH)
        count += 1
    pl.semaphore_wait(barrier, count)


def push(src, dst, sems, slot, where):
    copy = pltpu.make_async_remote_copy(
        src_ref=src, dst_ref=dst, send_sem=sems.at[(0,) + slot], recv_sem=sems.at[(1,) + slot],
        device_id=where, device_id_type=MESH)
    copy.start()
    return copy


def carry_kernel(m_ref, alog_ref, r_ref, recv, decay, line, band_send, band_recv, out, back, sem_there, sem_band, sem_back):
    tile = lax.axis_index("tile")
    rev = lax.axis_index("dir")
    row, col = tile // 8, tile % 8
    peers = tile_peers(tile)
    greet(peers[0] + peers[1])
    turn = lambda i, last: rev * last + (1 - 2 * rev) * i
    place = ((col, row), (row, col))
    there, bands, backs = [], [], []
    for axis in range(2):
        pos = place[axis][0]
        slot = turn(pos, 7)
        there.append([
            push(m_ref.at[axis, lax.rem(pos + d, 8)], recv.at[axis, slot], sem_there, (axis, d - 1), {"tile": peers[axis][d - 1]})
            for d in range(1, 8)])
        recv[axis, slot] = m_ref[axis, pos]

    def rate_of(axis, i):
        pos = place[axis][0]
        return -LOG2E * jnp.exp(alog_ref[axis, pl.ds(2 * pos + i, 1), :])

    for axis in range(2):
        for copy in there[axis]:
            copy.wait_recv()
        total = recv[axis, 0, 4]
        for tau in range(1, 8):
            total = total + recv[axis, tau, 4]
        for i in range(2):
            rate = rate_of(axis, i)

            def along(tau, state, axis=axis, i=i, rate=rate):
                d = jnp.exp2(recv[axis, tau, 4] * rate)
                decay[axis, i, tau] = d
                return d * state + recv[axis, tau, i]

            line[axis, i] = lax.fori_loop(0, 8, along, jnp.zeros((TS, E), jnp.float32))

            def against(k, state, axis=axis, i=i):
                tau = 7 - k
                return decay[axis, i, tau] * state + recv[axis, tau, 2 + i]

            line[axis, 2 + i] = lax.fori_loop(0, 8, against, jnp.zeros((TS, E), jnp.float32))
            line[axis, 4 + i] = jnp.exp2(total * rate)

        def fold(k, state, axis=axis):
            h0, h1, g0, g1 = state
            fw = pl.ds(turn(k, 15), 1)
            bw = pl.ds(turn(15 - k, 15), 1)
            return (line[axis, 4, fw, :] * h0 + line[axis, 0, fw, :], line[axis, 5, fw, :] * h1 + line[axis, 1, fw, :],
                    line[axis, 4, bw, :] * g0 + line[axis, 2, bw, :], line[axis, 5, bw, :] * g1 + line[axis, 3, bw, :])

        ends = lax.fori_loop(0, TS, fold, (jnp.zeros((1, E), jnp.float32),) * 4)
        for i in range(4):
            band_send[axis, i : i + 1, :] = ends[i]
        band_send[axis, 4:5, :] = jnp.sum(total, axis=0, keepdims=True)
        band_send[axis, 5:8, :] = jnp.zeros((3, E), jnp.float32)
        bslot = turn(place[axis][1], 7)
        bands.append([
            push(band_send.at[axis], band_recv.at[axis, bslot], sem_band, (axis, d - 1), {"tile": peers[1 - axis][d - 1]})
            for d in range(1, 8)])
        band_recv[axis, bslot] = band_send[axis]
    for axis in range(2):
        for copy in bands[axis]:
            copy.wait_recv()
        pos, band = place[axis]
        mine = turn(band, 7)
        starts = []
        for i in range(2):
            rate = rate_of(axis, i)

            def ahead(tau, state, axis=axis, i=i, rate=rate):
                grown = jnp.exp2(band_recv[axis, tau, 4:5, :] * rate) * state + band_recv[axis, tau, i : i + 1, :]
                return jnp.where(tau < mine, grown, state)

            def behind(k, state, axis=axis, i=i, rate=rate):
                tau = 7 - k
                grown = jnp.exp2(band_recv[axis, tau, 4:5, :] * rate) * state + band_recv[axis, tau, 2 + i : 3 + i, :]
                return jnp.where(tau > mine, grown, state)

            zero = jnp.zeros((1, E), jnp.float32)
            starts.append(lax.fori_loop(0, 8, ahead, zero))
            starts.append(lax.fori_loop(0, 8, behind, zero))

        def advance(k, state, axis=axis):
            h0, h1, g0, g1 = state
            fw = pl.ds(turn(k, 15), 1)
            bw = pl.ds(turn(15 - k, 15), 1)
            new = (line[axis, 4, fw, :] * h0 + line[axis, 0, fw, :], line[axis, 5, fw, :] * h1 + line[axis, 1, fw, :],
                   line[axis, 4, bw, :] * g0 + line[axis, 2, bw, :], line[axis, 5, bw, :] * g1 + line[axis, 3, bw, :])
            line[axis, 0, fw, :] = h0
            line[axis, 1, fw, :] = h1
            line[axis, 2, bw, :] = g0
            line[axis, 3, bw, :] = g1
            return new

        lax.fori_loop(0, TS, advance, (starts[0], starts[2], starts[1], starts[3]))
        for i in range(2):
            def entry(tau, state, axis=axis, i=i):
                out[axis, tau, i] = state
                return decay[axis, i, tau] * state + recv[axis, tau, i]

            lax.fori_loop(0, 8, entry, line[axis, i])

            def leave(k, state, axis=axis, i=i):
                tau = 7 - k
                out[axis, tau, 2 + i] = state
                return decay[axis, i, tau] * state + recv[axis, tau, 2 + i]

            lax.fori_loop(0, 8, leave, line[axis, 2 + i])
        backs.append([
            push(out.at[axis, turn(lax.rem(pos + d, 8), 7)], back.at[axis, pos], sem_back, (axis, d - 1), {"tile": peers[axis][d - 1]})
            for d in range(1, 8)])
        back[axis, pos] = out[axis, turn(pos, 7)]
    for axis in range(2):
        for copy in backs[axis]:
            copy.wait_recv()
        r_ref[axis] = back[axis]
    for copy in there[0] + there[1] + bands[0] + bands[1] + backs[0] + backs[1]:
        copy.wait_send()


def combine_kernel(y_ref, du_ref, dx_ref, yo_ref, duo_ref, dxo_ref,
                   half_buf, out_buf, dx_one, dx_two, dx_mid, dx_all, sem_half, sem_out, sem_dx):
    tile = lax.axis_index("tile")
    side = lax.axis_index("dir")
    other = 1 - side
    row, col = tile // 8, tile % 8
    along_row, along_col = tile_peers(tile)
    greet(along_row + along_col, other)
    partner = {"dir": other}
    parts = (y_ref, du_ref)
    there = [push(parts[k].at[other], half_buf.at[k], sem_half, (k,), partner) for k in range(2)]
    first = [push(dx_ref.at[lax.rem(col + d, 8)], dx_one.at[col], sem_dx, (0, d - 1), {"tile": along_row[d - 1]}) for d in range(1, 8)]
    dx_one[col] = dx_ref[col]
    for copy in first:
        copy.wait_recv()
    dx_two[row] = sum(dx_one[j] for j in range(8))
    second = [push(dx_two.at[row], dx_two.at[row], sem_dx, (1, d - 1), {"tile": along_col[d - 1]}) for d in range(1, 8)]
    for copy in second:
        copy.wait_recv()
    dx_all[col] = sum(dx_two[j] for j in range(8))
    third = [push(dx_all.at[col], dx_all.at[col], sem_dx, (2, d - 1), {"tile": along_row[d - 1]}) for d in range(1, 8)]
    backs = []
    for k in range(2):
        there[k].wait_recv()
        out_buf[k, side] = (parts[k][side] + half_buf[k]).astype(jnp.bfloat16)
        backs.append(push(out_buf.at[k, side], out_buf.at[k, side], sem_out, (k,), partner))
    for copy in third:
        copy.wait_recv()
    dxo_ref[...] = dx_all[...]
    backs[0].wait_recv()
    yo_ref[...] = out_buf[0]
    backs[1].wait_recv()
    duo_ref[...] = out_buf[1]
    for copy in there + first + second + third + backs:
        copy.wait_send()


def carries(maps, alog):
    dma = pltpu.SemaphoreType.DMA
    return pl.pallas_call(
        carry_kernel,
        out_shape=f32(2, 8, 4, TS, E),
        in_specs=[VMEM] * 2,
        out_specs=VMEM,
        scratch_shapes=[
            pltpu.VMEM((2, 8, 5, TS, E), jnp.float32),
            pltpu.VMEM((2, 2, 8, TS, E), jnp.float32),
            pltpu.VMEM((2, 6, TS, E), jnp.float32),
            pltpu.VMEM((2, 8, E), jnp.float32),
            pltpu.VMEM((2, 8, 8, E), jnp.float32),
            pltpu.VMEM((2, 8, 4, TS, E), jnp.float32),
            pltpu.VMEM((2, 8, 4, TS, E), jnp.float32),
            dma((2, 2, 7)), dma((2, 2, 7)), dma((2, 2, 7)),
        ],
        compiler_params=pltpu.CompilerParams(vmem_limit_bytes=48 * 2**20, collective_id=0, has_side_effects=True),
        name="carries",
    )(maps, alog)


def combine(y, du, dx):
    dma = pltpu.SemaphoreType.DMA
    half = jax.ShapeDtypeStruct((2, 128, E), jnp.bfloat16)
    return pl.pallas_call(
        combine_kernel,
        out_shape=(half, half, f32(8, TS, E)),
        in_specs=[VMEM] * 3,
        out_specs=(VMEM,) * 3,
        scratch_shapes=[
            pltpu.VMEM((2, 128, E), jnp.float32),
            pltpu.VMEM((2, 2, 128, E), jnp.bfloat16),
            pltpu.VMEM((8, TS, E), jnp.float32),
            pltpu.VMEM((8, TS, E), jnp.float32),
            pltpu.VMEM((8, TS, E), jnp.float32),
            pltpu.VMEM((8, TS, E), jnp.float32),
            dma((2, 2)), dma((2, 2)), dma((2, 3, 7)),
        ],
        compiler_params=pltpu.CompilerParams(vmem_limit_bytes=48 * 2**20, collective_id=1, has_side_effects=True),
        name="combine",
    )(y, du, dx)


def local(tiles, cotangent, xproj_w, dtproj_w, dt_bias, a_log, skip_d):
    x = tiles.reshape(TOK, E)
    cot = cotangent.reshape(TOK, E)
    rev = lax.axis_index("dir").astype(jnp.int32).reshape(1)
    xw = jnp.pad(xproj_w[0], ((0, 0), (0, 0), (0, 84)))
    dw = jnp.pad(dtproj_w[0], ((0, 0), (0, 116), (0, 0)))
    common = (rev, x, cot, xw, dw, dt_bias[0], a_log[0])
    entering = carries(line_maps(*common), a_log[0])
    y, du, dx = finish(*common, skip_d[0], entering)
    yo, duo, dxo = combine(y.reshape(2, 128, E), du.reshape(2, 128, E), dx.reshape(8, TS, E))
    dxo = dxo.reshape(2, 64, E)[:, :44].transpose(0, 2, 1)
    return yo.reshape(tiles.shape), duo.reshape(tiles.shape), dxo[None]


def solution(mesh):
    by_tile = P(("scene", "tile"), None, None, None)
    by_dir = P("dir", None, None, None)
    return jax.shard_map(
        local,
        mesh=mesh,
        in_specs=(by_tile, by_tile, by_dir, by_dir, P("dir", None, None), by_dir, P("dir", None, None)),
        out_specs=(by_tile, by_tile, P(("scene", "dir"), None, None, None)),
        check_vma=False,
    )
```

```python
import jax
import jax.numpy as jnp
from jax import lax
from jax.experimental import pallas as pl
from jax.experimental.pallas import tpu as pltpu
from jax.sharding import PartitionSpec as P

MESH = pl.DeviceIdType.MESH

E = 384
NS = 16
TS = 16
TOK = 256
LOG2E = 1.4426950408889634
LN2 = 0.6931471805599453
NT = (((1,), (1,)), ((), ()))
TN = (((0,), (0,)), ((), ()))
NN = (((1,), (0,)), ((), ()))


def dot(lhs, rhs, dims=NN):
    return lax.dot_general(lhs, rhs, dims, preferred_element_type=jnp.float32)


def halves(vals):
    top = vals.astype(jnp.bfloat16)
    return top, (vals - top.astype(jnp.float32)).astype(jnp.bfloat16)


def thirds(vals):
    top = vals.astype(jnp.bfloat16)
    rest = vals - top.astype(jnp.float32)
    return (top,) + halves(rest)


def swap_matrix():
    row = lax.broadcasted_iota(jnp.int32, (TOK, TOK), 0)
    col = lax.broadcasted_iota(jnp.int32, (TOK, TOK), 1)
    return ((row % TS) * TS + row // TS == col).astype(jnp.bfloat16)


def rounded(vals):
    return vals.astype(jnp.bfloat16).astype(jnp.float32)


def lane_block(et):
    return slice(et * 128, (et + 1) * 128)


def prepare(axis, io, sc):
    if axis == 0:
        swap = swap_matrix()
        xs = dot(swap, io.x[...])
        cs = dot(swap, io.cot[...])
        xb = xs.astype(jnp.bfloat16)
        sc.xb[...] = xb
    else:
        xb = io.x[...]
        xs = xb.astype(jnp.float32)
        cs = io.cot[...].astype(jnp.float32)
    sc.u[axis] = xs
    sc.cot[axis] = cs
    mixed = dot(xb, io.xw[axis])
    for n in range(2 * NS):
        sc.bc[axis, :, lane_block(n)] = jnp.broadcast_to(mixed[:, 12 + n : 13 + n], (TOK, 128))
    proj = io.dw[axis]
    raw = sum(dot(part, proj) for part in thirds(mixed))
    raw = raw + io.bias[axis : axis + 1, :]
    dt = jnp.maximum(raw, 0.0) + jnp.log1p(jnp.exp(-jnp.abs(raw)))
    sc.dt[axis] = dt
    sc.w[axis] = dt * xs
    sc.rate[axis] = -LOG2E * jnp.exp(io.alog[axis])
    size = dt[0:TS]
    for p in range(1, TS):
        size = size + dt[p * TS : (p + 1) * TS]
    sc.size[...] = size


def local_maps(axis, turn, sc):
    def unit(lh, carry):
        line0 = pl.multiple_of(lh * 8, 8)
        for et in range(3):
            lanes = lane_block(et)
            for half in range(2):
                ns = range(half * 8, half * 8 + 8)
                rates = [jnp.broadcast_to(sc.rate[axis, n : n + 1, lanes], (8, 128)) for n in ns]

                def step(t, state):
                    hs, qs, gs = state
                    rows = pl.ds(pl.multiple_of(turn(t, 15) * TS + line0, 8), 8)
                    dt = sc.dt[axis, rows, lanes]
                    w = sc.w[axis, rows, lanes]
                    ct = sc.cot[axis, rows, lanes]
                    nh, nq, ng = [], [], []
                    for m, n in enumerate(ns):
                        a = jnp.exp2(dt * rates[m])
                        nh.append(a * hs[m] + w * sc.bc[axis, rows, lane_block(n)])
                        q = a * qs[m]
                        nq.append(q)
                        ng.append(gs[m] + q * (sc.bc[axis, rows, lane_block(NS + n)] * ct))
                    return nh, nq, ng

                zero = [jnp.zeros((8, 128), jnp.float32)] * 8
                one = [jnp.ones((8, 128), jnp.float32)] * 8
                hs, qs, gs = lax.fori_loop(0, TS, step, (zero, one, zero))
                for m, n in enumerate(ns):
                    rows = pl.ds(pl.multiple_of(n * TS + line0, 8), 8)
                    sc.vals[0, et, rows, :] = hs[m]
                    sc.vals[1, et, rows, :] = gs[m]
        return carry

    lax.fori_loop(0, 2, unit, 0)

    def feed(k, state):
        out = []
        for sense in range(2):
            line = turn(k if sense == 0 else 15 - k, 15)
            size = 8.0 * sc.size[pl.ds(line, 1), :]
            for et in range(3):
                at = pl.ds(line, NS, stride=TS)
                decay = jnp.exp2(size[:, lane_block(et)] * sc.rate[axis, :, lane_block(et)])
                val = sc.vals[sense, et, at, :] + state[sense * 3 + et] * decay
                sent = rounded(val)
                sc.vals[sense, et, at, :] = sent
                out.append(val - sent)
        return out

    lax.fori_loop(0, TS, feed, [jnp.zeros((NS, 128), jnp.float32)] * 6)
    size = sc.size[...].astype(jnp.bfloat16)
    for j in range(8):
        for k in range(4):
            n = 2 * j + k % 2
            for et in range(3):
                sc.msg[axis, j, k, :, lane_block(et)] = sc.vals[k // 2, et, n * TS : (n + 1) * TS, :].astype(jnp.bfloat16)
        sc.msg[axis, j, 4] = size


def fold_lines(axis, pos, turn, sc):
    total = sc.recv[axis, 0, 4].astype(jnp.float32)
    for et in range(3):
        sc.before[axis, et, 0:TS, :] = jnp.zeros((TS, 128), jnp.float32)
    for tau in range(1, 8):
        for et in range(3):
            sc.before[axis, et, tau * TS : (tau + 1) * TS, :] = total[:, lane_block(et)]
        total = total + sc.recv[axis, tau, 4].astype(jnp.float32)
    sc.total[axis] = total
    for i in range(2):
        rate = sc.rate[axis, pl.ds(2 * pos + i, 1), :]

        def along(tau, state):
            d = jnp.exp2(sc.recv[axis, tau, 4].astype(jnp.float32) * rate)
            sc.decay[axis, i, tau] = d
            return d * state + sc.recv[axis, tau, i].astype(jnp.float32)

        sc.line[axis, i] = lax.fori_loop(0, 8, along, jnp.zeros((TS, E), jnp.float32))

        def against(k, state):
            tau = 7 - k
            return sc.decay[axis, i, tau] * state + sc.recv[axis, tau, 2 + i].astype(jnp.float32)

        sc.line[axis, 2 + i] = lax.fori_loop(0, 8, against, jnp.zeros((TS, E), jnp.float32))
        sc.line[axis, 4 + i] = jnp.exp2(total * rate)

    def fold(k, state):
        h0, h1, g0, g1 = state
        fw = pl.ds(turn(k, 15), 1)
        bw = pl.ds(turn(15 - k, 15), 1)
        return (sc.line[axis, 4, fw, :] * h0 + sc.line[axis, 0, fw, :], sc.line[axis, 5, fw, :] * h1 + sc.line[axis, 1, fw, :],
                sc.line[axis, 4, bw, :] * g0 + sc.line[axis, 2, bw, :], sc.line[axis, 5, bw, :] * g1 + sc.line[axis, 3, bw, :])

    ends = lax.fori_loop(0, TS, fold, (jnp.zeros((1, E), jnp.float32),) * 4)
    for i in range(4):
        sc.band_send[axis, i : i + 1, :] = ends[i]
    sc.band_send[axis, 4:5, :] = jnp.sum(total, axis=0, keepdims=True)
    sc.band_send[axis, 5:8, :] = jnp.zeros((3, E), jnp.float32)


def enter_lines(axis, pos, mine, turn, sc):
    zero = jnp.zeros((1, E), jnp.float32)
    rates = [sc.rate[axis, pl.ds(2 * pos + i, 1), :] for i in range(2)]
    starts = []
    for i in range(2):

        def ahead(tau, state):
            grown = jnp.exp2(sc.band_recv[axis, tau, 4:5, :] * rates[i]) * state + sc.band_recv[axis, tau, i : i + 1, :]
            return jnp.where(tau < mine, grown, state)

        def behind(k, state):
            tau = 7 - k
            grown = jnp.exp2(sc.band_recv[axis, tau, 4:5, :] * rates[i]) * state + sc.band_recv[axis, tau, 2 + i : 3 + i, :]
            return jnp.where(tau > mine, grown, state)

        starts.append((lax.fori_loop(0, 8, ahead, zero), lax.fori_loop(0, 8, behind, zero)))

    def advance(k, state):
        h0, h1, g0, g1 = state
        fw = pl.ds(turn(k, 15), 1)
        bw = pl.ds(turn(15 - k, 15), 1)
        new = (sc.line[axis, 4, fw, :] * h0 + sc.line[axis, 0, fw, :], sc.line[axis, 5, fw, :] * h1 + sc.line[axis, 1, fw, :],
               sc.line[axis, 4, bw, :] * g0 + sc.line[axis, 2, bw, :], sc.line[axis, 5, bw, :] * g1 + sc.line[axis, 3, bw, :])
        sc.line[axis, 0, fw, :] = h0
        sc.line[axis, 1, fw, :] = h1
        sc.line[axis, 2, bw, :] = g0
        sc.line[axis, 3, bw, :] = g1
        return new

    lax.fori_loop(0, TS, advance, (starts[0][0], starts[1][0], starts[0][1], starts[1][1]))

    def entry(tau, state):
        back = 7 - tau
        fw = pl.ds(pl.multiple_of(tau * TS, TS), TS)
        bw = pl.ds(pl.multiple_of(back * TS, TS), TS)
        for et in range(3):
            for i in range(2):
                sc.ent[i, et, fw, :] = state[i][:, lane_block(et)]
                sc.ent[2 + i, et, bw, :] = state[2 + i][:, lane_block(et)]
        return ([sc.decay[axis, i, tau] * state[i] + sc.recv[axis, tau, i].astype(jnp.float32) for i in range(2)]
                + [sc.decay[axis, i, back] * state[2 + i] + sc.recv[axis, back, 2 + i].astype(jnp.float32) for i in range(2)])

    lax.fori_loop(0, 8, entry, [sc.line[axis, k] for k in range(4)])

    def differ(k, state):
        out = []
        for et in range(3):
            lanes = lane_block(et)
            for sense in range(2):
                line = turn(k if sense == 0 else 15 - k, 15)
                at = pl.ds(line, 8, stride=TS)
                first = sc.before[axis, et, at, :]
                whole = sc.total[axis, pl.ds(line, 1), :][:, lanes]
                if sense == 1:
                    first = first + sc.own_f32[axis, et, at, :]
                    gap = state[6 * et + 3] + (whole - first)
                    left = first
                else:
                    gap = state[6 * et] + first
                    left = whole - first
                out.append(left)
                for i in range(2):
                    val = sc.ent[2 * sense + i, et, at, :]
                    guess = jnp.exp2(gap * rates[i][:, lanes]) * state[6 * et + 3 * sense + 1 + i]
                    sent = rounded(val - guess)
                    sc.ent[2 * sense + i, et, at, :] = sent
                    out.append(guess + sent)
        return out

    lax.fori_loop(0, TS, differ, [jnp.zeros((8, 128), jnp.float32)] * 18)
    for tau in range(8):
        for k in range(4):
            for et in range(3):
                sc.out[axis, tau, k, :, lane_block(et)] = sc.ent[k, et, tau * TS : (tau + 1) * TS, :].astype(jnp.bfloat16)


def decode(axis, slot, turn, sc):
    for j in range(8):
        for k in range(4):
            n = 2 * j + k % 2
            for et in range(3):
                sc.vals[k // 2, et, n * TS : (n + 1) * TS, :] = sc.back[axis, j, k, :, lane_block(et)].astype(jnp.float32)

    def add(k, state):
        out = []
        for et in range(3):
            lanes = lane_block(et)
            for sense in range(2):
                line = turn(k if sense == 0 else 15 - k, 15)
                own = pl.ds(slot * TS + line, 1)
                at = pl.ds(line, NS, stride=TS)
                first = sc.before[axis, et, own, :]
                whole = sc.total[axis, pl.ds(line, 1), :][:, lanes]
                if sense == 1:
                    first = first + sc.own_f32[axis, et, own, :]
                    gap = state[4 * et + 2] + (whole - first)
                    left = first
                else:
                    gap = state[4 * et] + first
                    left = whole - first
                val = jnp.exp2(gap * sc.rate[axis, :, lanes]) * state[4 * et + 2 * sense + 1] + sc.vals[sense, et, at, :]
                sc.vals[sense, et, at, :] = val
                out.append(left)
                out.append(val)
        return out

    lax.fori_loop(0, TS, add, [jnp.zeros((1, 128), jnp.float32), jnp.zeros((NS, 128), jnp.float32)] * 6)


def scan_tile(axis, turn, io, sc, sent_part):
    for et in range(3):
        lanes = lane_block(et)

        def unit(lh, carry):
            line0 = pl.multiple_of(lh * 8, 8)
            rates = [jnp.broadcast_to(sc.rate[axis, n : n + 1, lanes], (8, 128)) for n in range(NS)]
            skip = jnp.broadcast_to(io.skip[axis : axis + 1, lanes], (8, 128))

            def rows_at(t):
                return pl.ds(pl.multiple_of(turn(t, 15) * TS + line0, 8), 8)

            def start(sense):
                return [sc.vals[sense, et, pl.ds(pl.multiple_of(n * TS + line0, 8), 8), :] for n in range(NS)]

            def forward(t, hs):
                rows = rows_at(t)
                dt = sc.dt[axis, rows, lanes]
                w = sc.w[axis, rows, lanes]
                ct = sc.cot[axis, rows, lanes]
                y = skip * sc.u[axis, rows, lanes]
                out = []
                for n in range(NS):
                    a = jnp.exp2(dt * rates[n])
                    ah = a * hs[n]
                    sc.ah[t, n] = ah
                    h = ah + w * sc.bc[axis, rows, lane_block(n)]
                    cols = lane_block(NS + n)
                    y = y + h * sc.bc[axis, rows, cols]
                    dc = h * ct
                    if et > 0:
                        dc = dc + sc.dbc[rows, cols]
                    sc.dbc[rows, cols] = dc
                    out.append(h)
                if axis == 0:
                    sc.turned[0, et, rows, :] = y
                else:
                    sc.field[0, et, rows, :] = sc.field[0, et, rows, :] + y
                return out

            lax.fori_loop(0, TS, forward, start(0))

            def backward(i, gs):
                t = 15 - i
                rows = rows_at(t)
                dt = sc.dt[axis, rows, lanes]
                w = sc.w[axis, rows, lanes]
                ct = sc.cot[axis, rows, lanes]
                dw = jnp.zeros((8, 128), jnp.float32)
                dr = jnp.zeros((8, 128), jnp.float32)
                out = []
                for n in range(NS):
                    a = jnp.exp2(dt * rates[n])
                    g = gs[n] + sc.bc[axis, rows, lane_block(NS + n)] * ct
                    cols = lane_block(n)
                    db = g * w
                    if et > 0:
                        db = db + sc.dbc[rows, cols]
                    sc.dbc[rows, cols] = db
                    dw = dw + g * sc.bc[axis, rows, cols]
                    dr = dr + (g * sc.ah[t, n]) * rates[n]
                    out.append(a * g)
                sc.ddt[rows, lanes] = dr * LN2 + dw * sc.u[axis, rows, lanes]
                du = dw * dt + skip * ct
                if axis == 0:
                    sc.turned[1, et, rows, :] = du
                else:
                    sc.field[1, et, rows, :] = sc.field[1, et, rows, :] + du
                return out

            lax.fori_loop(0, TS, backward, start(1))
            return carry

        lax.fori_loop(0, 2, unit, 0)
        sent_part(et)


def project_back(axis, io, sc):
    dt = sc.dt[axis]
    small = dt * (1.0 - dt * (0.5 - dt * (1.0 / 6.0 - dt * (1.0 / 24.0))))
    dv = sc.ddt[...] * jnp.where(dt < 0.03, small, 1.0 - jnp.exp(-dt))
    proj = io.dw[axis]
    dmix = sum(dot(part, proj, NT) for part in halves(dv))
    row = lax.broadcasted_iota(jnp.int32, (512, 128), 0)
    col = lax.broadcasted_iota(jnp.int32, (512, 128), 1)
    for blk in range(8):
        pick = (col == 12 + blk * 4 + row // 128).astype(jnp.bfloat16)
        for part in halves(sc.dbc[:, blk * 512 : (blk + 1) * 512]):
            dmix = dmix + dot(part, pick)
    parts = halves(dmix)
    weight = io.xw[axis]
    xb = sc.xb[...] if axis == 0 else io.x[...]
    dx = sum(dot(part, xb, TN) for part in parts)
    for q in range(4):
        sc.dx_src[4 * axis + q] = dx[q * TS : (q + 1) * TS]
    return sum(dot(part, weight, NT) for part in parts)


class Refs:
    def __init__(self, names, refs):
        self.__dict__.update(zip(names, refs))


INPUTS = ("x", "cot", "xw", "dw", "bias", "alog", "skip")


def layer_kernel(*refs):
    hbm = refs[:7]
    yo_ref, duo_ref, dxo_ref = refs[7:10]
    sc = Refs(SCRATCH, refs[10:])
    io = Refs(INPUTS, [getattr(sc, "in_" + name) for name in INPUTS])
    tile = lax.axis_index("tile")
    side = lax.axis_index("dir")
    other = 1 - side
    row, col = tile // 8, tile % 8
    along_row = [row * 8 + lax.rem(col + d, 8) for d in range(1, 8)]
    along_col = [lax.rem(row + d, 8) * 8 + col for d in range(1, 8)]
    peers = (along_row, along_col)
    place = ((col, row), (row, col))
    partner = {"dir": other}

    def turn(i, last):
        return side * last + (1 - 2 * side) * i

    barrier = pltpu.get_barrier_semaphore()
    for peer in along_row + along_col:
        pl.semaphore_signal(barrier, inc=1, device_id={"tile": peer}, device_id_type=MESH)
    pl.semaphore_signal(barrier, inc=1, device_id=partner, device_id_type=MESH)
    loads = [pltpu.make_async_copy(hbm[k], getattr(sc, "in_" + name), sc.sem_in.at[k]) for k, name in enumerate(INPUTS)]
    for load in loads:
        load.start()
    for load in loads:
        load.wait()

    def push(src, dst, sems, slot, where):
        copy = pltpu.make_async_remote_copy(
            src_ref=src, dst_ref=dst, send_sem=sems.at[(0,) + slot], recv_sem=sems.at[(1,) + slot],
            device_id=where, device_id_type=MESH)
        copy.start()
        return copy

    there, bands, backs = [], [], []
    for axis in range(2):
        prepare(axis, io, sc)
        local_maps(axis, turn, sc)
        if axis == 0:
            pl.semaphore_wait(barrier, 15)
        pos = place[axis][0]
        slot = turn(pos, 7)
        there.append([
            push(sc.msg.at[axis, lax.rem(pos + d, 8)], sc.recv.at[axis, slot], sc.sem_there, (axis, d - 1), {"tile": peers[axis][d - 1]})
            for d in range(1, 8)])
        sc.recv[axis, slot] = sc.msg[axis, pos]
    for axis in range(2):
        pos, band = place[axis]
        for copy in there[axis]:
            copy.wait_recv()
        for tau in range(8):
            for et in range(3):
                sc.own_f32[axis, et, tau * TS : (tau + 1) * TS, :] = sc.recv[axis, tau, 4, :, lane_block(et)].astype(jnp.float32)
        fold_lines(axis, pos, turn, sc)
        slot = turn(band, 7)
        bands.append([
            push(sc.band_send.at[axis], sc.band_recv.at[axis, slot], sc.sem_band, (axis, d - 1), {"tile": peers[1 - axis][d - 1]})
            for d in range(1, 8)])
        sc.band_recv[axis, slot] = sc.band_send[axis]
    for axis in range(2):
        pos, band = place[axis]
        for copy in bands[axis]:
            copy.wait_recv()
        enter_lines(axis, pos, turn(band, 7), turn, sc)
        backs.append([
            push(sc.out.at[axis, turn(lax.rem(pos + d, 8), 7)], sc.back.at[axis, pos], sc.sem_back, (axis, d - 1), {"tile": peers[axis][d - 1]})
            for d in range(1, 8)])
        sc.back[axis, pos] = sc.out[axis, turn(pos, 7)]

    halves_sent = [[], []]
    other_rows = pl.ds(pl.multiple_of(other * 128, 128), 128)
    own_rows = pl.ds(pl.multiple_of(side * 128, 128), 128)

    def send_half(kind, et):
        halves_sent[kind].append(push(sc.field.at[kind, et, other_rows, :], sc.half.at[kind, et], sc.sem_half, (kind, et), partner))

    for axis in range(2):
        for copy in backs[axis]:
            copy.wait_recv()
        decode(axis, turn(place[axis][0], 7), turn, sc)
        scan_tile(axis, turn, io, sc, (lambda et: None) if axis == 0 else (lambda et: send_half(0, et)))
        through = project_back(axis, io, sc)
        for et in range(3):
            if axis == 0:
                sc.turned[1, et] = sc.turned[1, et] + through[:, lane_block(et)]
                for kind in range(2):
                    for i in range(TS):
                        sc.field[kind, et, i * TS : (i + 1) * TS, :] = sc.turned[kind, et, pl.ds(i, TS, stride=TS), :]
            else:
                sc.field[1, et] = sc.field[1, et] + through[:, lane_block(et)]
                send_half(1, et)
    first = [push(sc.dx_src.at[lax.rem(col + d, 8)], sc.dx_one.at[col], sc.sem_dx, (0, d - 1), {"tile": along_row[d - 1]}) for d in range(1, 8)]
    sc.dx_one[col] = sc.dx_src[col]
    outs = []

    def merge(kind):
        for et in range(3):
            halves_sent[kind][et].wait_recv()
            sc.res[kind, own_rows, lane_block(et)] = (sc.field[kind, et, own_rows, :] + sc.half[kind, et]).astype(jnp.bfloat16)
        outs.append(push(sc.res.at[kind, own_rows, :], sc.res.at[kind, own_rows, :], sc.sem_out, (kind,), partner))

    merge(0)
    for copy in first:
        copy.wait_recv()
    sc.dx_two[row] = sum(sc.dx_one[j] for j in range(8))
    second = [push(sc.dx_two.at[row], sc.dx_two.at[row], sc.sem_dx, (1, d - 1), {"tile": along_col[d - 1]}) for d in range(1, 8)]
    merge(1)
    for copy in second:
        copy.wait_recv()
    sc.dx_all[col] = sum(sc.dx_two[j] for j in range(8))
    third = [push(sc.dx_all.at[col], sc.dx_all.at[col], sc.sem_dx, (2, d - 1), {"tile": along_row[d - 1]}) for d in range(1, 8)]
    outs[0].wait_recv()
    yo_ref[...] = sc.res[0]
    for copy in third:
        copy.wait_recv()
    dxo_ref[...] = sc.dx_all[...]
    outs[1].wait_recv()
    duo_ref[...] = sc.res[1]
    for group in there + bands + backs + halves_sent + [outs, first, second, third]:
        for copy in group:
            copy.wait_send()


def f32_buf(*shape):
    return pltpu.VMEM(shape, jnp.float32)


def bf16_buf(*shape):
    return pltpu.VMEM(shape, jnp.bfloat16)


def dma_sems(*shape):
    return pltpu.SemaphoreType.DMA(shape)


BUFFERS = {
    "in_x": bf16_buf(TOK, E), "in_cot": bf16_buf(TOK, E), "in_xw": bf16_buf(2, E, 128), "in_dw": bf16_buf(2, 128, E),
    "in_bias": f32_buf(2, E), "in_alog": f32_buf(2, NS, E), "in_skip": f32_buf(2, E), "sem_in": dma_sems(7),
    "xb": bf16_buf(TOK, E),
    "u": f32_buf(2, TOK, E), "cot": f32_buf(2, TOK, E), "dt": f32_buf(2, TOK, E), "w": f32_buf(2, TOK, E),
    "bc": f32_buf(2, TOK, 4096), "rate": f32_buf(2, NS, E), "size": f32_buf(TS, E),
    "vals": f32_buf(2, 3, NS * TS, 128),
    "msg": bf16_buf(2, 8, 5, TS, E), "recv": bf16_buf(2, 8, 5, TS, E),
    "before": f32_buf(2, 3, 8 * TS, 128), "own_f32": f32_buf(2, 3, 8 * TS, 128), "total": f32_buf(2, TS, E),
    "decay": f32_buf(2, 2, 8, TS, E), "line": f32_buf(2, 6, TS, E),
    "band_send": f32_buf(2, 8, E), "band_recv": f32_buf(2, 8, 8, E),
    "ent": f32_buf(4, 3, 8 * TS, 128),
    "out": bf16_buf(2, 8, 4, TS, E), "back": bf16_buf(2, 8, 4, TS, E),
    "dbc": f32_buf(TOK, 4096), "ah": f32_buf(TS, NS, 8, 128), "ddt": f32_buf(TOK, E),
    "turned": f32_buf(2, 3, TOK, 128), "field": f32_buf(2, 3, TOK, 128),
    "half": f32_buf(2, 3, 128, 128), "res": bf16_buf(2, TOK, E),
    "dx_src": f32_buf(8, TS, E), "dx_one": f32_buf(8, TS, E), "dx_two": f32_buf(8, TS, E), "dx_all": f32_buf(8, TS, E),
    "sem_there": dma_sems(2, 2, 7), "sem_band": dma_sems(2, 2, 7), "sem_back": dma_sems(2, 2, 7),
    "sem_half": dma_sems(2, 2, 3), "sem_out": dma_sems(2, 2), "sem_dx": dma_sems(2, 3, 7),
}
SCRATCH = tuple(BUFFERS)
VMEM = pl.BlockSpec(memory_space=pltpu.VMEM)


def local(tiles, cotangent, xproj_w, dtproj_w, dt_bias, a_log, skip_d):
    xw = jnp.pad(xproj_w[0], ((0, 0), (0, 0), (0, 84)))
    dw = jnp.pad(dtproj_w[0], ((0, 0), (0, 116), (0, 0)))
    out = jax.ShapeDtypeStruct((TOK, E), jnp.bfloat16)
    yo, duo, dxo = pl.pallas_call(
        layer_kernel,
        out_shape=(out, out, jax.ShapeDtypeStruct((8, TS, E), jnp.float32)),
        in_specs=[pl.BlockSpec(memory_space=pl.ANY)] * 7,
        out_specs=(VMEM,) * 3,
        scratch_shapes=list(BUFFERS.values()),
        compiler_params=pltpu.CompilerParams(vmem_limit_bytes=56 * 2**20, collective_id=0, has_side_effects=True),
        name="layer",
    )(tiles.reshape(TOK, E), cotangent.reshape(TOK, E), xw, dw, dt_bias[0], a_log[0], skip_d[0])
    dxo = dxo.reshape(2, 64, E)[:, :44].transpose(0, 2, 1)
    return yo.reshape(tiles.shape), duo.reshape(tiles.shape), dxo[None]


def solution(mesh):
    by_tile = P(("scene", "tile"), None, None, None)
    by_dir = P("dir", None, None, None)
    return jax.shard_map(
        local,
        mesh=mesh,
        in_specs=(by_tile, by_tile, by_dir, by_dir, P("dir", None, None), by_dir, P("dir", None, None)),
        out_specs=(by_tile, by_tile, P(("scene", "dir"), None, None, None)),
        check_vma=False,
    )
```

```python
import jax
import jax.numpy as jnp
from jax import lax
from jax.experimental import pallas as pl
from jax.experimental.pallas import tpu as pltpu
from jax.sharding import PartitionSpec as P

MESH = pl.DeviceIdType.MESH

E = 384
NS = 16
TS = 16
TOK = 256
LOG2E = 1.4426950408889634
LN2 = 0.6931471805599453
NT = (((1,), (1,)), ((), ()))
TN = (((0,), (0,)), ((), ()))
NN = (((1,), (0,)), ((), ()))


def dot(lhs, rhs, dims=NN):
    return lax.dot_general(lhs, rhs, dims, preferred_element_type=jnp.float32)


def halves(vals):
    top = vals.astype(jnp.bfloat16)
    return top, (vals - top.astype(jnp.float32)).astype(jnp.bfloat16)


def thirds(vals):
    top = vals.astype(jnp.bfloat16)
    rest = vals - top.astype(jnp.float32)
    return (top,) + halves(rest)


def swap_matrix():
    row = lax.broadcasted_iota(jnp.int32, (TOK, TOK), 0)
    col = lax.broadcasted_iota(jnp.int32, (TOK, TOK), 1)
    return ((row % TS) * TS + row // TS == col).astype(jnp.bfloat16)


def rounded(vals):
    return vals.astype(jnp.bfloat16).astype(jnp.float32)


def lane_block(et):
    return slice(et * 128, (et + 1) * 128)


def prepare(axis, io, sc):
    if axis == 0:
        swap = swap_matrix()
        xs = dot(swap, io.x[...])
        cs = dot(swap, io.cot[...])
        xb = xs.astype(jnp.bfloat16)
    else:
        xb = io.x[...]
        xs = xb.astype(jnp.float32)
        cs = io.cot[...].astype(jnp.float32)
    sc.u[axis] = xs.reshape(TS, TS, E)
    sc.cot[axis] = cs.reshape(TS, TS, E)
    for given, kept, count in ((io.xw, sc.xw, 44), (io.dw, sc.dw, 12)):
        sc.padded[...] = jnp.zeros((128, E), jnp.float32)
        sc.padded[0:count, :] = given[...].astype(jnp.float32)[:, axis, :]
        kept[axis] = sc.padded[...].astype(jnp.bfloat16)
    mixed = dot(xb, sc.xw[axis], NT)
    for n in range(2 * NS):
        sc.bc[axis, :, :, lane_block(n)] = jnp.broadcast_to(mixed[:, 12 + n : 13 + n], (TOK, 128)).reshape(TS, TS, 128)
    proj = sc.dw[axis]
    raw = sum(dot(part, proj) for part in thirds(mixed))
    raw = raw + io.bias[axis : axis + 1, :]
    dt = jnp.maximum(raw, 0.0) + jnp.log1p(jnp.exp(-jnp.abs(raw)))
    sc.dt[axis] = dt.reshape(TS, TS, E)
    sc.w[axis] = (dt * xs).reshape(TS, TS, E)
    sc.rate[axis] = -LOG2E * jnp.exp(io.alog[axis])
    size = dt[0:TS]
    for p in range(1, TS):
        size = size + dt[p * TS : (p + 1) * TS]
    sc.size[...] = size


def local_maps(axis, half, turn, sc):
    ns = range(half * 8, half * 8 + 8)

    def unit(lh, carry):
        line0 = pl.multiple_of(lh * 8, 8)
        lines = pl.ds(line0, 8)
        for et in range(3):
            lanes = lane_block(et)
            rates = [jnp.broadcast_to(sc.rate[axis, n : n + 1, lanes], (8, 128)) for n in ns]

            def step(t, state):
                hs, qs, gs = state
                p = turn(t, 15)
                dt = sc.dt[axis, p, lines, lanes]
                w = sc.w[axis, p, lines, lanes]
                ct = sc.cot[axis, p, lines, lanes]
                nh, nq, ng = [], [], []
                for m, n in enumerate(ns):
                    a = jnp.exp2(dt * rates[m])
                    nh.append(a * hs[m] + w * sc.bc[axis, p, lines, lane_block(n)])
                    q = a * qs[m]
                    nq.append(q)
                    ng.append(gs[m] + q * (sc.bc[axis, p, lines, lane_block(NS + n)] * ct))
                return nh, nq, ng

            zero = [jnp.zeros((8, 128), jnp.float32)] * 8
            one = [jnp.ones((8, 128), jnp.float32)] * 8
            hs, qs, gs = lax.fori_loop(0, TS, step, (zero, one, zero))
            for m, n in enumerate(ns):
                rows = pl.ds(pl.multiple_of(n * TS + line0, 8), 8)
                sc.vals[axis, 0, et, rows, :] = hs[m]
                sc.vals[axis, 1, et, rows, :] = gs[m]
        return carry

    lax.fori_loop(0, 2, unit, 0)

    def feed(k, state):
        out = []
        for sense in range(2):
            line = turn(k if sense == 0 else 15 - k, 15)
            size = 8.0 * sc.size[pl.ds(line, 1), :]
            for et in range(3):
                at = pl.ds(half * 8 * TS + line, 8, stride=TS)
                decay = jnp.exp2(size[:, lane_block(et)] * sc.rate[axis, half * 8 : half * 8 + 8, lane_block(et)])
                val = sc.vals[axis, sense, et, at, :] + state[sense * 3 + et] * decay
                sent = rounded(val)
                sc.vals[axis, sense, et, at, :] = sent
                out.append(val - sent)
        return out

    lax.fori_loop(0, TS, feed, [jnp.zeros((8, 128), jnp.float32)] * 6)
    size = sc.size[...].astype(jnp.bfloat16)
    for j in range(half * 4, half * 4 + 4):
        for k in range(4):
            n = 2 * j + k % 2
            for et in range(3):
                sc.msg[axis, j, k, :, lane_block(et)] = sc.vals[axis, k // 2, et, n * TS : (n + 1) * TS, :].astype(jnp.bfloat16)
        sc.msg[axis, j, 4] = size


def fold_lines(axis, pos, turn, sc):
    total = sc.recv[axis, 0, 4].astype(jnp.float32)
    for et in range(3):
        sc.before[axis, et, 0:TS, :] = jnp.zeros((TS, 128), jnp.float32)
    for tau in range(1, 8):
        for et in range(3):
            sc.before[axis, et, tau * TS : (tau + 1) * TS, :] = total[:, lane_block(et)]
        total = total + sc.recv[axis, tau, 4].astype(jnp.float32)
    sc.total[axis] = total
    for i in range(2):
        rate = sc.rate[axis, pl.ds(2 * pos + i, 1), :]

        def along(tau, state):
            d = jnp.exp2(sc.recv[axis, tau, 4].astype(jnp.float32) * rate)
            sc.decay[axis, i, tau] = d
            return d * state + sc.recv[axis, tau, i].astype(jnp.float32)

        sc.line[axis, i] = lax.fori_loop(0, 8, along, jnp.zeros((TS, E), jnp.float32))

        def against(k, state):
            tau = 7 - k
            return sc.decay[axis, i, tau] * state + sc.recv[axis, tau, 2 + i].astype(jnp.float32)

        sc.line[axis, 2 + i] = lax.fori_loop(0, 8, against, jnp.zeros((TS, E), jnp.float32))
        sc.line[axis, 4 + i] = jnp.exp2(total * rate)

    def fold(k, state):
        h0, h1, g0, g1 = state
        fw = pl.ds(turn(k, 15), 1)
        bw = pl.ds(turn(15 - k, 15), 1)
        return (sc.line[axis, 4, fw, :] * h0 + sc.line[axis, 0, fw, :], sc.line[axis, 5, fw, :] * h1 + sc.line[axis, 1, fw, :],
                sc.line[axis, 4, bw, :] * g0 + sc.line[axis, 2, bw, :], sc.line[axis, 5, bw, :] * g1 + sc.line[axis, 3, bw, :])

    ends = lax.fori_loop(0, TS, fold, (jnp.zeros((1, E), jnp.float32),) * 4)
    for i in range(4):
        sc.band_send[axis, i : i + 1, :] = ends[i]
    sc.band_send[axis, 4:5, :] = jnp.sum(total, axis=0, keepdims=True)
    sc.band_send[axis, 5:8, :] = jnp.zeros((3, E), jnp.float32)


def enter_lines(axis, pos, mine, turn, sc):
    zero = jnp.zeros((1, E), jnp.float32)
    rates = [sc.rate[axis, pl.ds(2 * pos + i, 1), :] for i in range(2)]
    starts = []
    for i in range(2):

        def ahead(tau, state):
            grown = jnp.exp2(sc.band_recv[axis, tau, 4:5, :] * rates[i]) * state + sc.band_recv[axis, tau, i : i + 1, :]
            return jnp.where(tau < mine, grown, state)

        def behind(k, state):
            tau = 7 - k
            grown = jnp.exp2(sc.band_recv[axis, tau, 4:5, :] * rates[i]) * state + sc.band_recv[axis, tau, 2 + i : 3 + i, :]
            return jnp.where(tau > mine, grown, state)

        starts.append((lax.fori_loop(0, 8, ahead, zero), lax.fori_loop(0, 8, behind, zero)))

    def advance(k, state):
        h0, h1, g0, g1 = state
        fw = pl.ds(turn(k, 15), 1)
        bw = pl.ds(turn(15 - k, 15), 1)
        new = (sc.line[axis, 4, fw, :] * h0 + sc.line[axis, 0, fw, :], sc.line[axis, 5, fw, :] * h1 + sc.line[axis, 1, fw, :],
               sc.line[axis, 4, bw, :] * g0 + sc.line[axis, 2, bw, :], sc.line[axis, 5, bw, :] * g1 + sc.line[axis, 3, bw, :])
        sc.line[axis, 0, fw, :] = h0
        sc.line[axis, 1, fw, :] = h1
        sc.line[axis, 2, bw, :] = g0
        sc.line[axis, 3, bw, :] = g1
        return new

    lax.fori_loop(0, TS, advance, (starts[0][0], starts[1][0], starts[0][1], starts[1][1]))

    def entry(tau, state):
        back = 7 - tau
        fw = pl.ds(pl.multiple_of(tau * TS, TS), TS)
        bw = pl.ds(pl.multiple_of(back * TS, TS), TS)
        for et in range(3):
            for i in range(2):
                sc.ent[i, et, fw, :] = state[i][:, lane_block(et)]
                sc.ent[2 + i, et, bw, :] = state[2 + i][:, lane_block(et)]
        return ([sc.decay[axis, i, tau] * state[i] + sc.recv[axis, tau, i].astype(jnp.float32) for i in range(2)]
                + [sc.decay[axis, i, back] * state[2 + i] + sc.recv[axis, back, 2 + i].astype(jnp.float32) for i in range(2)])

    lax.fori_loop(0, 8, entry, [sc.line[axis, k] for k in range(4)])

    def differ(k, state):
        out = []
        for et in range(3):
            lanes = lane_block(et)
            for sense in range(2):
                line = turn(k if sense == 0 else 15 - k, 15)
                at = pl.ds(line, 8, stride=TS)
                first = sc.before[axis, et, at, :]
                whole = sc.total[axis, pl.ds(line, 1), :][:, lanes]
                if sense == 1:
                    first = first + sc.own_f32[axis, et, at, :]
                    gap = state[6 * et + 3] + (whole - first)
                    left = first
                else:
                    gap = state[6 * et] + first
                    left = whole - first
                out.append(left)
                for i in range(2):
                    val = sc.ent[2 * sense + i, et, at, :]
                    guess = jnp.exp2(gap * rates[i][:, lanes]) * state[6 * et + 3 * sense + 1 + i]
                    sent = rounded(val - guess)
                    sc.ent[2 * sense + i, et, at, :] = sent
                    out.append(guess + sent)
        return out

    lax.fori_loop(0, TS, differ, [jnp.zeros((8, 128), jnp.float32)] * 18)
    for tau in range(8):
        for k in range(4):
            for et in range(3):
                sc.out[axis, tau, k, :, lane_block(et)] = sc.ent[k, et, tau * TS : (tau + 1) * TS, :].astype(jnp.bfloat16)


def decode(axis, slot, turn, sc):
    for j in range(8):
        for k in range(4):
            n = 2 * j + k % 2
            for et in range(3):
                sc.vals[axis, k // 2, et, n * TS : (n + 1) * TS, :] = sc.back[axis, j, k, :, lane_block(et)].astype(jnp.float32)

    def add(k, state):
        out = []
        for et in range(3):
            lanes = lane_block(et)
            for sense in range(2):
                line = turn(k if sense == 0 else 15 - k, 15)
                own = pl.ds(slot * TS + line, 1)
                at = pl.ds(line, NS, stride=TS)
                first = sc.before[axis, et, own, :]
                whole = sc.total[axis, pl.ds(line, 1), :][:, lanes]
                if sense == 1:
                    first = first + sc.own_f32[axis, et, own, :]
                    gap = state[4 * et + 2] + (whole - first)
                    left = first
                else:
                    gap = state[4 * et] + first
                    left = whole - first
                val = jnp.exp2(gap * sc.rate[axis, :, lanes]) * state[4 * et + 2 * sense + 1] + sc.vals[axis, sense, et, at, :]
                sc.vals[axis, sense, et, at, :] = val
                out.append(left)
                out.append(val)
        return out

    lax.fori_loop(0, TS, add, [jnp.zeros((1, 128), jnp.float32), jnp.zeros((NS, 128), jnp.float32)] * 6)


def scan_forward(axis, et, lh, turn, io, sc):
    line0 = pl.multiple_of(lh * 8, 8)
    lines = pl.ds(line0, 8)
    lanes = lane_block(et)
    rates = [jnp.broadcast_to(sc.rate[axis, n : n + 1, lanes], (8, 128)) for n in range(NS)]
    skip = jnp.broadcast_to(io.skip[axis : axis + 1, lanes], (8, 128))

    def forward(t, hs):
        p = turn(t, 15)
        dt = sc.dt[axis, p, lines, lanes]
        w = sc.w[axis, p, lines, lanes]
        ct = sc.cot[axis, p, lines, lanes]
        y = skip * sc.u[axis, p, lines, lanes]
        out = []
        for n in range(NS):
            a = jnp.exp2(dt * rates[n])
            ah = a * hs[n]
            sc.ah[axis, et, lh, t, n] = ah
            h = ah + w * sc.bc[axis, p, lines, lane_block(n)]
            cols = lane_block(NS + n)
            y = y + h * sc.bc[axis, p, lines, cols]
            dc = h * ct
            if et > 0:
                dc = dc + sc.dbc[axis, p, lines, cols]
            sc.dbc[axis, p, lines, cols] = dc
            out.append(h)
        if axis == 0:
            sc.turned[0, et, pl.ds(pl.multiple_of(p * TS + line0, 8), 8), :] = y
        else:
            sc.field[0, et, p, lines, :] = sc.field[0, et, p, lines, :] + y
        return out

    lax.fori_loop(0, TS, forward, [sc.vals[axis, 0, et, pl.ds(pl.multiple_of(n * TS + line0, 8), 8), :] for n in range(NS)])


def scan_backward(axis, et, lh, turn, io, sc):
    line0 = pl.multiple_of(lh * 8, 8)
    lines = pl.ds(line0, 8)
    lanes = lane_block(et)
    rates = [jnp.broadcast_to(sc.rate[axis, n : n + 1, lanes], (8, 128)) for n in range(NS)]
    skip = jnp.broadcast_to(io.skip[axis : axis + 1, lanes], (8, 128))

    def backward(i, gs):
        t = 15 - i
        p = turn(t, 15)
        dt = sc.dt[axis, p, lines, lanes]
        w = sc.w[axis, p, lines, lanes]
        ct = sc.cot[axis, p, lines, lanes]
        dw = jnp.zeros((8, 128), jnp.float32)
        dr = jnp.zeros((8, 128), jnp.float32)
        out = []
        for n in range(NS):
            a = jnp.exp2(dt * rates[n])
            g = gs[n] + sc.bc[axis, p, lines, lane_block(NS + n)] * ct
            cols = lane_block(n)
            db = g * w
            if et > 0:
                db = db + sc.dbc[axis, p, lines, cols]
            sc.dbc[axis, p, lines, cols] = db
            dw = dw + g * sc.bc[axis, p, lines, cols]
            dr = dr + (g * sc.ah[axis, et, lh, t, n]) * rates[n]
            out.append(a * g)
        sc.ddt[axis, p, lines, lanes] = dr * LN2 + dw * sc.u[axis, p, lines, lanes]
        du = dw * dt + skip * ct
        if axis == 0:
            sc.turned[1, et, pl.ds(pl.multiple_of(p * TS + line0, 8), 8), :] = du
        else:
            sc.field[1, et, p, lines, :] = sc.field[1, et, p, lines, :] + du
        return out

    lax.fori_loop(0, TS, backward, [sc.vals[axis, 1, et, pl.ds(pl.multiple_of(n * TS + line0, 8), 8), :] for n in range(NS)])


def project_back(axis, lines, count, io, sc):
    rows = TS * count
    dt = sc.dt[axis, :, lines, :].reshape(rows, E)
    small = dt * (1.0 - dt * (0.5 - dt * (1.0 / 6.0 - dt * (1.0 / 24.0))))
    dv = sc.ddt[axis, :, lines, :].reshape(rows, E) * jnp.where(dt < 0.03, small, 1.0 - jnp.exp(-dt))
    proj = sc.dw[axis]
    dmix = sum(dot(part, proj, NT) for part in halves(dv))
    row = lax.broadcasted_iota(jnp.int32, (512, 128), 0)
    col = lax.broadcasted_iota(jnp.int32, (512, 128), 1)
    for blk in range(8):
        pick = (col == 12 + blk * 4 + row // 128).astype(jnp.bfloat16)
        for part in halves(sc.dbc[axis, :, lines, blk * 512 : (blk + 1) * 512].reshape(rows, 512)):
            dmix = dmix + dot(part, pick)
    parts = halves(dmix)
    weight = sc.xw[axis]
    xb = sc.u[axis, :, lines, :].reshape(rows, E).astype(jnp.bfloat16)
    return sum(dot(part, xb, TN) for part in parts), sum(dot(part, weight) for part in parts)


class Refs:
    def __init__(self, names, refs):
        self.__dict__.update(zip(names, refs))


INPUTS = ("x", "cot", "xw", "dw", "bias", "alog", "skip")


def layer_kernel(*refs):
    hbm = refs[:7]
    yo_ref, duo_ref, dxo_ref = refs[7:10]
    sc = Refs(SCRATCH, refs[10:])
    io = Refs(INPUTS, [getattr(sc, "in_" + name) for name in INPUTS])
    tile = lax.axis_index("tile")
    side = lax.axis_index("dir")
    other = 1 - side
    row, col = tile // 8, tile % 8
    along_row = [row * 8 + lax.rem(col + d, 8) for d in range(1, 8)]
    along_col = [lax.rem(row + d, 8) * 8 + col for d in range(1, 8)]
    peers = (along_row, along_col)
    depth, plane = tile // 16, tile % 16
    in_plane = [depth * 16 + lax.rem(plane + d, 16) for d in range(1, 16)]
    in_depth = [lax.rem(depth + d, 4) * 16 + plane for d in range(1, 4)]
    beside = (1 - row % 2 + 2 * depth) * 8
    others_near = [beside + lax.rem(col + d, 8) for d in range(1, 8)]
    place = ((col, row), (row, col))
    partner = {"dir": other}

    def turn(i, last):
        return side * last + (1 - 2 * side) * i

    barrier = pltpu.get_barrier_semaphore()
    for peer in along_row + along_col + others_near:
        pl.semaphore_signal(barrier, inc=1, device_id={"tile": peer}, device_id_type=MESH)
    pl.semaphore_signal(barrier, inc=1, device_id=partner, device_id_type=MESH)
    loads = [pltpu.make_async_copy(hbm[k], getattr(sc, "in_" + name), sc.sem_in.at[k]) for k, name in enumerate(INPUTS)]
    for load in loads:
        load.start()
    for load in loads:
        load.wait()

    def push(src, dst, sems, slot, where):
        copy = pltpu.make_async_remote_copy(
            src_ref=src, dst_ref=dst, send_sem=sems.at[(0,) + slot], recv_sem=sems.at[(1,) + slot],
            device_id=where, device_id_type=MESH)
        copy.start()
        return copy

    bands, backs = [[], []], [[], []]

    def map_copy(axis, share, sender, where):
        return pltpu.make_async_remote_copy(
            src_ref=sc.msg.at[axis, share], dst_ref=sc.recv.at[axis, turn(sender, 7)],
            send_sem=sc.sem_there.at[0, axis, share], recv_sem=sc.sem_there.at[1, axis, sender],
            device_id=where, device_id_type=MESH)

    def send_maps(axis):
        pos = place[axis][0]
        sc.recv[axis, turn(pos, 7)] = sc.msg[axis, pos]
        for d in range(1, 8):
            map_copy(axis, lax.rem(pos + d, 8), pos, {"tile": peers[axis][d - 1]}).start()

    def wait_maps(axis, sent):
        pos = place[axis][0]
        for d in range(1, 8):
            peer = lax.rem(pos + d, 8)
            copy = map_copy(axis, peer if sent else 0, pos if sent else peer, {"tile": peers[axis][d - 1]})
            if sent:
                copy.wait_send()
            else:
                copy.wait_recv()

    def fold_and_send(axis):
        pos, band = place[axis]
        wait_maps(axis, False)
        for tau in range(8):
            for et in range(3):
                sc.own_f32[axis, et, tau * TS : (tau + 1) * TS, :] = sc.recv[axis, tau, 4, :, lane_block(et)].astype(jnp.float32)
        fold_lines(axis, pos, turn, sc)
        slot = turn(band, 7)
        bands[axis] = [
            push(sc.band_send.at[axis], sc.band_recv.at[axis, slot], sc.sem_band, (axis, d - 1), {"tile": peers[1 - axis][d - 1]})
            for d in range(1, 8)]
        sc.band_recv[axis, slot] = sc.band_send[axis]

    def enter_and_send(axis):
        pos, band = place[axis]
        for copy in bands[axis]:
            copy.wait_recv()
        enter_lines(axis, pos, turn(band, 7), turn, sc)
        backs[axis] = [
            push(sc.out.at[axis, turn(lax.rem(pos + d, 8), 7)], sc.back.at[axis, pos], sc.sem_back, (axis, d - 1), {"tile": peers[axis][d - 1]})
            for d in range(1, 8)]
        sc.back[axis, pos] = sc.out[axis, turn(pos, 7)]

    prepare(0, io, sc)
    local_maps(0, 0, turn, sc)
    pl.semaphore_wait(barrier, 22)
    local_maps(0, 1, turn, sc)
    send_maps(0)
    prepare(1, io, sc)
    local_maps(1, 0, turn, sc)
    local_maps(1, 1, turn, sc)
    fold_and_send(0)
    send_maps(1)
    enter_and_send(0)
    fold_and_send(1)
    enter_and_send(1)

    halves_sent = [[], []]
    own = pl.ds(pl.multiple_of(side * 8, 8), 8)
    others = pl.ds(pl.multiple_of(other * 8, 8), 8)

    def send_half(kind):
        for et in range(3):
            halves_sent[kind].append(push(sc.field.at[kind, et, :, others, :], sc.half.at[kind, et], sc.sem_half, (kind, et), partner))

    def dx_put(axis, dx):
        for j in range(16):
            sc.dx_src[j, 4 * axis : 4 * axis + 4] = dx[3 * j : 3 * j + 4]

    def dx_first():
        sc.dx_one[plane] = sc.dx_src[plane]
        return [push(sc.dx_src.at[lax.rem(plane + d, 16)], sc.dx_one.at[plane], sc.sem_dx, (0, d - 1), {"tile": in_plane[d - 1]})
                for d in range(1, 16)]

    def dx_next(arriving, phase):
        for copy in arriving:
            copy.wait_recv()
        if phase == 1:
            sc.dx_two[depth] = sum(sc.dx_one[j] for j in range(16))
            part, there = sc.dx_two.at[depth], in_depth
        else:
            sc.dx_all[plane] = sum(sc.dx_two[j] for j in range(4))
            part, there = sc.dx_all.at[plane], in_plane
        return [push(part, part, sc.sem_dx, (phase, k), {"tile": tile_to}) for k, tile_to in enumerate(there)]

    outs = []

    def merge(kind):
        for et in range(3):
            halves_sent[kind][et].wait_recv()
            total = sc.field[kind, et, :, own, :] + sc.half[kind, et]
            sc.res[kind, et, side] = total.reshape(128, 128).astype(jnp.bfloat16)
            outs.append(push(sc.res.at[kind, et, side], sc.res.at[kind, et, side], sc.sem_out, (kind, et), partner))

    def write_out(kind, ref):
        for et in range(3):
            outs[3 * kind + et].wait_recv()
            parts = [sc.res[kind, et, h].astype(jnp.float32).reshape(TS, 8, 128) for h in range(2)]
            ref[:, lane_block(et)] = jnp.concatenate(parts, axis=1).reshape(TOK, 128).astype(jnp.bfloat16)

    def both(fn, axis):
        def unit(lh, carry):
            for et in range(3):
                fn(axis, et, lh, turn, io, sc)
            return carry

        lax.fori_loop(0, 2, unit, 0)

    def to_field(kind):
        for et in range(3):
            for i in range(TS):
                sc.field[kind, et, i] = sc.turned[kind, et, pl.ds(i, TS, stride=TS), :]

    for copy in backs[0]:
        copy.wait_recv()
    decode(0, turn(col, 7), turn, sc)
    both(scan_forward, 0)
    to_field(0)
    for copy in backs[1]:
        copy.wait_recv()
    decode(1, turn(row, 7), turn, sc)
    for et in range(3):
        scan_forward(1, et, other, turn, io, sc)
    send_half(0)
    both(scan_backward, 0)
    dx, through = project_back(0, slice(0, TS), TS, io, sc)
    dx_put(0, dx)
    for et in range(3):
        sc.turned[1, et] = sc.turned[1, et] + through[:, lane_block(et)]
    to_field(1)
    dxs = []
    for lh, lines in ((other, others), (side, own)):
        if lh is side:
            for et in range(3):
                scan_forward(1, et, side, turn, io, sc)
            merge(0)
        for et in range(3):
            scan_backward(1, et, lh, turn, io, sc)
        dx, through = project_back(1, lines, 8, io, sc)
        dxs.append(dx)
        for et in range(3):
            sc.field[1, et, :, lines, :] = sc.field[1, et, :, lines, :] + through[:, lane_block(et)].reshape(TS, 8, 128)
        if lh is other:
            send_half(1)
    dx_put(1, dxs[0] + dxs[1])
    dx_sent = [dx_first()]
    dx_sent.append(dx_next(dx_sent[0], 1))
    merge(1)
    dx_sent.append(dx_next(dx_sent[1], 2))
    write_out(0, yo_ref)
    for copy in dx_sent[2]:
        copy.wait_recv()
    for j in range(15):
        for axis in range(2):
            count = min(3, 44 - 3 * j)
            dxo_ref[3 * j : 3 * j + count, axis, :] = sc.dx_all[j, 4 * axis : 4 * axis + count, :]
    write_out(1, duo_ref)
    for axis in range(2):
        wait_maps(axis, True)
    for group in bands + backs + halves_sent + [outs] + dx_sent:
        for copy in group:
            copy.wait_send()


def f32_buf(*shape):
    return pltpu.VMEM(shape, jnp.float32)


def bf16_buf(*shape):
    return pltpu.VMEM(shape, jnp.bfloat16)


def dma_sems(*shape):
    return pltpu.SemaphoreType.DMA(shape)


BUFFERS = {
    "in_x": bf16_buf(TOK, E), "in_cot": bf16_buf(TOK, E), "in_xw": bf16_buf(44, 2, E), "in_dw": bf16_buf(12, 2, E), "padded": f32_buf(128, E), "xw": bf16_buf(2, 128, E), "dw": bf16_buf(2, 128, E),
    "in_bias": f32_buf(2, E), "in_alog": f32_buf(2, NS, E), "in_skip": f32_buf(2, E), "sem_in": dma_sems(7),
    "u": f32_buf(2, TS, TS, E), "cot": f32_buf(2, TS, TS, E), "dt": f32_buf(2, TS, TS, E), "w": f32_buf(2, TS, TS, E),
    "bc": f32_buf(2, TS, TS, 4096), "rate": f32_buf(2, NS, E), "size": f32_buf(TS, E),
    "vals": f32_buf(2, 2, 3, NS * TS, 128),
    "msg": bf16_buf(2, 8, 5, TS, E), "recv": bf16_buf(2, 8, 5, TS, E),
    "before": f32_buf(2, 3, 8 * TS, 128), "own_f32": f32_buf(2, 3, 8 * TS, 128), "total": f32_buf(2, TS, E),
    "decay": f32_buf(2, 2, 8, TS, E), "line": f32_buf(2, 6, TS, E),
    "band_send": f32_buf(2, 8, E), "band_recv": f32_buf(2, 8, 8, E),
    "ent": f32_buf(4, 3, 8 * TS, 128),
    "out": bf16_buf(2, 8, 4, TS, E), "back": bf16_buf(2, 8, 4, TS, E),
    "dbc": f32_buf(2, TS, TS, 4096), "ah": f32_buf(2, 3, 2, TS, NS, 8, 128), "ddt": f32_buf(2, TS, TS, E),
    "turned": f32_buf(2, 3, TOK, 128), "field": f32_buf(2, 3, TS, TS, 128),
    "half": f32_buf(2, 3, TS, 8, 128), "res": bf16_buf(2, 3, 2, 128, 128),
    "dx_src": f32_buf(16, 8, E), "dx_one": f32_buf(16, 8, E), "dx_two": f32_buf(4, 8, E), "dx_all": f32_buf(16, 8, E),
    "sem_there": dma_sems(2, 2, 8), "sem_band": dma_sems(2, 2, 7), "sem_back": dma_sems(2, 2, 7),
    "sem_half": dma_sems(2, 2, 3), "sem_out": dma_sems(2, 2, 3), "sem_dx": dma_sems(2, 3, 15),
}
SCRATCH = tuple(BUFFERS)
VMEM = pl.BlockSpec(memory_space=pltpu.VMEM)


def local(tiles, cotangent, xproj_w, dtproj_w, dt_bias, a_log, skip_d):
    xw = xproj_w[0].transpose(2, 0, 1)
    dw = dtproj_w[0].transpose(1, 0, 2)
    out = jax.ShapeDtypeStruct((TOK, E), jnp.bfloat16)
    yo, duo, dxo = pl.pallas_call(
        layer_kernel,
        out_shape=(out, out, jax.ShapeDtypeStruct((44, 2, E), jnp.float32)),
        in_specs=[pl.BlockSpec(memory_space=pl.ANY)] * 7,
        out_specs=(VMEM,) * 3,
        scratch_shapes=list(BUFFERS.values()),
        compiler_params=pltpu.CompilerParams(vmem_limit_bytes=56 * 2**20, collective_id=0, has_side_effects=True),
        name="layer",
    )(tiles.reshape(TOK, E), cotangent.reshape(TOK, E), xw, dw, dt_bias[0], a_log[0], skip_d[0])
    return yo.reshape(tiles.shape), duo.reshape(tiles.shape), dxo.transpose(1, 2, 0)[None]


def solution(mesh):
    by_tile = P(("scene", "tile"), None, None, None)
    by_dir = P("dir", None, None, None)
    return jax.shard_map(
        local,
        mesh=mesh,
        in_specs=(by_tile, by_tile, by_dir, by_dir, P("dir", None, None), by_dir, P("dir", None, None)),
        out_specs=(by_tile, by_tile, P(("scene", "dir"), None, None, None)),
        check_vma=False,
    )
```

```python
import jax
import jax.numpy as jnp
from jax import lax
from jax.experimental import pallas as pl
from jax.experimental.pallas import tpu as pltpu
from jax.sharding import PartitionSpec as P

MESH = pl.DeviceIdType.MESH

E = 384
NS = 16
TS = 16
TOK = 256
LOG2E = 1.4426950408889634
LN2 = 0.6931471805599453
NT = (((1,), (1,)), ((), ()))
TN = (((0,), (0,)), ((), ()))
NN = (((1,), (0,)), ((), ()))


def dot(lhs, rhs, dims=NN):
    return lax.dot_general(lhs, rhs, dims, preferred_element_type=jnp.float32)


def halves(vals):
    top = vals.astype(jnp.bfloat16)
    return top, (vals - top.astype(jnp.float32)).astype(jnp.bfloat16)


def thirds(vals):
    top = vals.astype(jnp.bfloat16)
    rest = vals - top.astype(jnp.float32)
    return (top,) + halves(rest)


def swap_matrix():
    row = lax.broadcasted_iota(jnp.int32, (TOK, TOK), 0)
    col = lax.broadcasted_iota(jnp.int32, (TOK, TOK), 1)
    return ((row % TS) * TS + row // TS == col).astype(jnp.bfloat16)


def rounded(vals):
    return vals.astype(jnp.bfloat16).astype(jnp.float32)


def lane_block(et):
    return slice(et * 128, (et + 1) * 128)


def prepare(axis, io, sc):
    if axis == 0:
        swap = swap_matrix()
        xs = dot(swap, io.x[...])
        cs = dot(swap, io.cot[...])
        xb = xs.astype(jnp.bfloat16)
    else:
        xb = io.x[...]
        xs = xb.astype(jnp.float32)
        cs = io.cot[...].astype(jnp.float32)
    sc.u[axis] = xs.reshape(TS, TS, E)
    sc.cot[axis] = cs.reshape(TS, TS, E)
    for given, kept, count in ((io.xw, sc.xw, 44), (io.dw, sc.dw, 12)):
        sc.padded[...] = jnp.zeros((128, E), jnp.float32)
        sc.padded[0:count, :] = given[...].astype(jnp.float32)[:, axis, :]
        kept[axis] = sc.padded[...].astype(jnp.bfloat16)
    mixed = dot(xb, sc.xw[axis], NT)
    for n in range(2 * NS):
        sc.bc[axis, :, :, lane_block(n)] = jnp.broadcast_to(mixed[:, 12 + n : 13 + n], (TOK, 128)).reshape(TS, TS, 128)
    proj = sc.dw[axis]
    raw = sum(dot(part, proj) for part in thirds(mixed))
    raw = raw + io.bias[axis : axis + 1, :]
    dt = jnp.maximum(raw, 0.0) + jnp.log1p(jnp.exp(-jnp.abs(raw)))
    sc.dt[axis] = dt.reshape(TS, TS, E)
    sc.w[axis] = (dt * xs).reshape(TS, TS, E)
    rate = -LOG2E * jnp.exp(io.alog[axis])
    sc.rate[axis] = rate
    for n in range(NS):
        sc.rate8[axis, n] = jnp.broadcast_to(rate[n : n + 1], (8, E))
    size = dt[0:TS]
    for p in range(1, TS):
        size = size + dt[p * TS : (p + 1) * TS]
    sc.size[...] = size


def local_maps(axis, half, turn, sc):
    ns = range(half * 8, half * 8 + 8)

    def unit(lh, carry):
        line0 = pl.multiple_of(lh * 8, 8)
        lines = pl.ds(line0, 8)
        for et in range(3):
            lanes = lane_block(et)
            rates = [jnp.broadcast_to(sc.rate[axis, n : n + 1, lanes], (8, 128)) for n in ns]

            def step(t, state):
                hs, qs, gs = state
                p = turn(t, 15)
                dt = sc.dt[axis, p, lines, lanes]
                w = sc.w[axis, p, lines, lanes]
                ct = sc.cot[axis, p, lines, lanes]
                nh, nq, ng = [], [], []
                for m, n in enumerate(ns):
                    a = jnp.exp2(dt * rates[m])
                    nh.append(a * hs[m] + w * sc.bc[axis, p, lines, lane_block(n)])
                    q = a * qs[m]
                    nq.append(q)
                    ng.append(gs[m] + q * (sc.bc[axis, p, lines, lane_block(NS + n)] * ct))
                return nh, nq, ng

            zero = [jnp.zeros((8, 128), jnp.float32)] * 8
            one = [jnp.ones((8, 128), jnp.float32)] * 8
            hs, qs, gs = lax.fori_loop(0, TS, step, (zero, one, zero))
            for m, n in enumerate(ns):
                rows = pl.ds(pl.multiple_of(n * TS + line0, 8), 8)
                sc.vals[axis, 0, et, rows, :] = hs[m]
                sc.vals[axis, 1, et, rows, :] = gs[m]
        return carry

    lax.fori_loop(0, 2, unit, 0)

    def feed(k, state):
        out = []
        for sense in range(2):
            line = turn(k if sense == 0 else 15 - k, 15)
            size = 8.0 * sc.size[pl.ds(line, 1), :]
            for et in range(3):
                at = pl.ds(half * 8 * TS + line, 8, stride=TS)
                decay = jnp.exp2(size[:, lane_block(et)] * sc.rate[axis, half * 8 : half * 8 + 8, lane_block(et)])
                val = sc.vals[axis, sense, et, at, :] + state[sense * 3 + et] * decay
                sent = rounded(val)
                sc.vals[axis, sense, et, at, :] = sent
                out.append(val - sent)
        return out

    lax.fori_loop(0, TS, feed, [jnp.zeros((8, 128), jnp.float32)] * 6)
    size = sc.size[...].astype(jnp.bfloat16)
    for j in range(half * 4, half * 4 + 4):
        for k in range(4):
            n = 2 * j + k % 2
            for et in range(3):
                sc.msg[axis, j, k, :, lane_block(et)] = sc.vals[axis, k // 2, et, n * TS : (n + 1) * TS, :].astype(jnp.bfloat16)
        sc.msg[axis, j, 4] = size


def fold_lines(axis, pos, turn, sc):
    total = sc.recv[axis, 0, 4].astype(jnp.float32)
    for et in range(3):
        sc.before[axis, et, 0:TS, :] = jnp.zeros((TS, 128), jnp.float32)
    for tau in range(1, 8):
        for et in range(3):
            sc.before[axis, et, tau * TS : (tau + 1) * TS, :] = total[:, lane_block(et)]
        total = total + sc.recv[axis, tau, 4].astype(jnp.float32)
    sc.total[axis] = total
    for i in range(2):
        rate = sc.rate[axis, pl.ds(2 * pos + i, 1), :]

        def along(tau, state):
            d = jnp.exp2(sc.recv[axis, tau, 4].astype(jnp.float32) * rate)
            sc.decay[axis, i, tau] = d
            return d * state + sc.recv[axis, tau, i].astype(jnp.float32)

        sc.line[axis, i] = lax.fori_loop(0, 8, along, jnp.zeros((TS, E), jnp.float32))

        def against(k, state):
            tau = 7 - k
            return sc.decay[axis, i, tau] * state + sc.recv[axis, tau, 2 + i].astype(jnp.float32)

        sc.line[axis, 2 + i] = lax.fori_loop(0, 8, against, jnp.zeros((TS, E), jnp.float32))
        sc.line[axis, 4 + i] = jnp.exp2(total * rate)

    def fold(k, state):
        h0, h1, g0, g1 = state
        fw = pl.ds(turn(k, 15), 1)
        bw = pl.ds(turn(15 - k, 15), 1)
        return (sc.line[axis, 4, fw, :] * h0 + sc.line[axis, 0, fw, :], sc.line[axis, 5, fw, :] * h1 + sc.line[axis, 1, fw, :],
                sc.line[axis, 4, bw, :] * g0 + sc.line[axis, 2, bw, :], sc.line[axis, 5, bw, :] * g1 + sc.line[axis, 3, bw, :])

    ends = lax.fori_loop(0, TS, fold, (jnp.zeros((1, E), jnp.float32),) * 4)
    for i in range(4):
        sc.band_send[axis, i : i + 1, :] = ends[i]
    sc.band_send[axis, 4:5, :] = jnp.sum(total, axis=0, keepdims=True)
    sc.band_send[axis, 5:8, :] = jnp.zeros((3, E), jnp.float32)


def enter_lines(axis, pos, mine, turn, sc):
    zero = jnp.zeros((1, E), jnp.float32)
    rates = [sc.rate[axis, pl.ds(2 * pos + i, 1), :] for i in range(2)]
    starts = []
    for i in range(2):

        def ahead(tau, state):
            grown = jnp.exp2(sc.band_recv[axis, tau, 4:5, :] * rates[i]) * state + sc.band_recv[axis, tau, i : i + 1, :]
            return jnp.where(tau < mine, grown, state)

        def behind(k, state):
            tau = 7 - k
            grown = jnp.exp2(sc.band_recv[axis, tau, 4:5, :] * rates[i]) * state + sc.band_recv[axis, tau, 2 + i : 3 + i, :]
            return jnp.where(tau > mine, grown, state)

        starts.append((lax.fori_loop(0, 8, ahead, zero), lax.fori_loop(0, 8, behind, zero)))

    def advance(k, state):
        h0, h1, g0, g1 = state
        fw = pl.ds(turn(k, 15), 1)
        bw = pl.ds(turn(15 - k, 15), 1)
        new = (sc.line[axis, 4, fw, :] * h0 + sc.line[axis, 0, fw, :], sc.line[axis, 5, fw, :] * h1 + sc.line[axis, 1, fw, :],
               sc.line[axis, 4, bw, :] * g0 + sc.line[axis, 2, bw, :], sc.line[axis, 5, bw, :] * g1 + sc.line[axis, 3, bw, :])
        sc.line[axis, 0, fw, :] = h0
        sc.line[axis, 1, fw, :] = h1
        sc.line[axis, 2, bw, :] = g0
        sc.line[axis, 3, bw, :] = g1
        return new

    lax.fori_loop(0, TS, advance, (starts[0][0], starts[1][0], starts[0][1], starts[1][1]))

    def entry(tau, state):
        back = 7 - tau
        fw = pl.ds(pl.multiple_of(tau * TS, TS), TS)
        bw = pl.ds(pl.multiple_of(back * TS, TS), TS)
        for et in range(3):
            for i in range(2):
                sc.ent[i, et, fw, :] = state[i][:, lane_block(et)]
                sc.ent[2 + i, et, bw, :] = state[2 + i][:, lane_block(et)]
        return ([sc.decay[axis, i, tau] * state[i] + sc.recv[axis, tau, i].astype(jnp.float32) for i in range(2)]
                + [sc.decay[axis, i, back] * state[2 + i] + sc.recv[axis, back, 2 + i].astype(jnp.float32) for i in range(2)])

    lax.fori_loop(0, 8, entry, [sc.line[axis, k] for k in range(4)])

    def differ(k, state):
        out = []
        for et in range(3):
            lanes = lane_block(et)
            for sense in range(2):
                line = turn(k if sense == 0 else 15 - k, 15)
                at = pl.ds(line, 8, stride=TS)
                first = sc.before[axis, et, at, :]
                whole = sc.total[axis, pl.ds(line, 1), :][:, lanes]
                if sense == 1:
                    first = first + sc.own_f32[axis, et, at, :]
                    gap = state[6 * et + 3] + (whole - first)
                    left = first
                else:
                    gap = state[6 * et] + first
                    left = whole - first
                out.append(left)
                for i in range(2):
                    val = sc.ent[2 * sense + i, et, at, :]
                    guess = jnp.exp2(gap * rates[i][:, lanes]) * state[6 * et + 3 * sense + 1 + i]
                    sent = rounded(val - guess)
                    sc.ent[2 * sense + i, et, at, :] = sent
                    out.append(guess + sent)
        return out

    lax.fori_loop(0, TS, differ, [jnp.zeros((8, 128), jnp.float32)] * 18)
    for tau in range(8):
        for k in range(4):
            for et in range(3):
                sc.out[axis, tau, k, :, lane_block(et)] = sc.ent[k, et, tau * TS : (tau + 1) * TS, :].astype(jnp.bfloat16)


def decode(axis, slot, turn, sc):
    for j in range(8):
        for k in range(4):
            n = 2 * j + k % 2
            for et in range(3):
                sc.vals[axis, k // 2, et, n * TS : (n + 1) * TS, :] = sc.back[axis, j, k, :, lane_block(et)].astype(jnp.float32)

    def add(k, state):
        out = []
        for et in range(3):
            lanes = lane_block(et)
            for sense in range(2):
                line = turn(k if sense == 0 else 15 - k, 15)
                own = pl.ds(slot * TS + line, 1)
                at = pl.ds(line, NS, stride=TS)
                first = sc.before[axis, et, own, :]
                whole = sc.total[axis, pl.ds(line, 1), :][:, lanes]
                if sense == 1:
                    first = first + sc.own_f32[axis, et, own, :]
                    gap = state[4 * et + 2] + (whole - first)
                    left = first
                else:
                    gap = state[4 * et] + first
                    left = whole - first
                val = jnp.exp2(gap * sc.rate[axis, :, lanes]) * state[4 * et + 2 * sense + 1] + sc.vals[axis, sense, et, at, :]
                sc.vals[axis, sense, et, at, :] = val
                out.append(left)
                out.append(val)
        return out

    lax.fori_loop(0, TS, add, [jnp.zeros((1, 128), jnp.float32), jnp.zeros((NS, 128), jnp.float32)] * 6)


def scan_forward(axis, lh, turn, io, sc):
    line0 = pl.multiple_of(lh * 8, 8)
    lines = pl.ds(line0, 8)
    for half in range(2):
        ns = range(half * 8, half * 8 + 8)

        def forward(t, hs):
            p = turn(t, 15)
            dt, w, ct, y = [], [], [], []
            for et in range(3):
                lanes = lane_block(et)
                dt.append(sc.dt[axis, p, lines, lanes])
                w.append(sc.w[axis, p, lines, lanes])
                ct.append(sc.cot[axis, p, lines, lanes])
                y.append(io.skip[axis : axis + 1, lanes] * sc.u[axis, p, lines, lanes] if half == 0 else jnp.zeros((8, 128), jnp.float32))
            out = []
            for m, n in enumerate(ns):
                b = sc.bc[axis, p, lines, lane_block(n)]
                c = sc.bc[axis, p, lines, lane_block(NS + n)]
                dc = jnp.zeros((8, 128), jnp.float32)
                for et in range(3):
                    a = jnp.exp2(dt[et] * sc.rate8[axis, n, :, lane_block(et)])
                    ah = a * hs[3 * m + et]
                    sc.ah[axis, et, lh, t, n] = ah
                    h = ah + w[et] * b
                    y[et] = y[et] + h * c
                    dc = dc + h * ct[et]
                    out.append(h)
                sc.dbc[axis, p, lines, lane_block(NS + n)] = dc
            for et in range(3):
                if axis == 0:
                    rows = pl.ds(pl.multiple_of(p * TS + line0, 8), 8)
                    sc.turned[0, et, rows, :] = y[et] if half == 0 else sc.turned[0, et, rows, :] + y[et]
                else:
                    sc.field[0, et, p, lines, :] = sc.field[0, et, p, lines, :] + y[et]
            return out

        start = [sc.vals[axis, 0, et, pl.ds(pl.multiple_of(n * TS + line0, 8), 8), :] for n in ns for et in range(3)]
        lax.fori_loop(0, TS, forward, start)


def scan_backward(axis, lh, turn, io, sc):
    line0 = pl.multiple_of(lh * 8, 8)
    lines = pl.ds(line0, 8)
    for half in range(2):
        ns = range(half * 8, half * 8 + 8)

        def backward(i, gs):
            t = 15 - i
            p = turn(t, 15)
            dt, w, ct, dw, dr = [], [], [], [], []
            for et in range(3):
                lanes = lane_block(et)
                dt.append(sc.dt[axis, p, lines, lanes])
                w.append(sc.w[axis, p, lines, lanes])
                ct.append(sc.cot[axis, p, lines, lanes])
                dw.append(jnp.zeros((8, 128), jnp.float32))
                dr.append(jnp.zeros((8, 128), jnp.float32))
            out = []
            for m, n in enumerate(ns):
                b = sc.bc[axis, p, lines, lane_block(n)]
                c = sc.bc[axis, p, lines, lane_block(NS + n)]
                db = jnp.zeros((8, 128), jnp.float32)
                for et in range(3):
                    rate = sc.rate8[axis, n, :, lane_block(et)]
                    g = gs[3 * m + et] + c * ct[et]
                    db = db + g * w[et]
                    dw[et] = dw[et] + g * b
                    dr[et] = dr[et] + (g * sc.ah[axis, et, lh, t, n]) * rate
                    out.append(jnp.exp2(dt[et] * rate) * g)
                sc.dbc[axis, p, lines, lane_block(n)] = db
            for et in range(3):
                lanes = lane_block(et)
                ddt = dr[et] * LN2 + dw[et] * sc.u[axis, p, lines, lanes]
                sc.ddt[axis, p, lines, lanes] = ddt if half == 0 else sc.ddt[axis, p, lines, lanes] + ddt
                du = dw[et] * dt[et]
                if half == 0:
                    du = du + io.skip[axis : axis + 1, lanes] * ct[et]
                if axis == 0:
                    rows = pl.ds(pl.multiple_of(p * TS + line0, 8), 8)
                    sc.turned[1, et, rows, :] = du if half == 0 else sc.turned[1, et, rows, :] + du
                else:
                    sc.field[1, et, p, lines, :] = sc.field[1, et, p, lines, :] + du
            return out

        start = [sc.vals[axis, 1, et, pl.ds(pl.multiple_of(n * TS + line0, 8), 8), :] for n in ns for et in range(3)]
        lax.fori_loop(0, TS, backward, start)


def project_back(axis, lines, count, io, sc):
    rows = TS * count
    dt = sc.dt[axis, :, lines, :].reshape(rows, E)
    small = dt * (1.0 - dt * (0.5 - dt * (1.0 / 6.0 - dt * (1.0 / 24.0))))
    dv = sc.ddt[axis, :, lines, :].reshape(rows, E) * jnp.where(dt < 0.03, small, 1.0 - jnp.exp(-dt))
    proj = sc.dw[axis]
    dmix = sum(dot(part, proj, NT) for part in halves(dv))
    row = lax.broadcasted_iota(jnp.int32, (512, 128), 0)
    col = lax.broadcasted_iota(jnp.int32, (512, 128), 1)
    for blk in range(8):
        pick = (col == 12 + blk * 4 + row // 128).astype(jnp.bfloat16)
        for part in halves(sc.dbc[axis, :, lines, blk * 512 : (blk + 1) * 512].reshape(rows, 512)):
            dmix = dmix + dot(part, pick)
    parts = halves(dmix)
    weight = sc.xw[axis]
    xb = sc.u[axis, :, lines, :].reshape(rows, E).astype(jnp.bfloat16)
    return sum(dot(part, xb, TN) for part in parts), sum(dot(part, weight) for part in parts)


class Refs:
    def __init__(self, names, refs):
        self.__dict__.update(zip(names, refs))


INPUTS = ("x", "cot", "xw", "dw", "bias", "alog", "skip")


def layer_kernel(*refs):
    hbm = refs[:7]
    yo_ref, duo_ref, dxo_ref = refs[7:10]
    sc = Refs(SCRATCH, refs[10:])
    io = Refs(INPUTS, [getattr(sc, "in_" + name) for name in INPUTS])
    tile = lax.axis_index("tile")
    side = lax.axis_index("dir")
    other = 1 - side
    row, col = tile // 8, tile % 8
    along_row = [row * 8 + lax.rem(col + d, 8) for d in range(1, 8)]
    along_col = [lax.rem(row + d, 8) * 8 + col for d in range(1, 8)]
    peers = (along_row, along_col)
    depth, plane = tile // 16, tile % 16
    in_plane = [depth * 16 + lax.rem(plane + d, 16) for d in range(1, 16)]
    in_depth = [lax.rem(depth + d, 4) * 16 + plane for d in range(1, 4)]
    beside = (1 - row % 2 + 2 * depth) * 8
    others_near = [beside + lax.rem(col + d, 8) for d in range(1, 8)]
    place = ((col, row), (row, col))
    partner = {"dir": other}

    def turn(i, last):
        return side * last + (1 - 2 * side) * i

    barrier = pltpu.get_barrier_semaphore()
    for peer in along_row + along_col + others_near:
        pl.semaphore_signal(barrier, inc=1, device_id={"tile": peer}, device_id_type=MESH)
    pl.semaphore_signal(barrier, inc=1, device_id=partner, device_id_type=MESH)
    loads = [pltpu.make_async_copy(hbm[k], getattr(sc, "in_" + name), sc.sem_in.at[k]) for k, name in enumerate(INPUTS)]
    for load in loads:
        load.start()
    for load in loads:
        load.wait()

    def push(src, dst, sems, slot, where):
        copy = pltpu.make_async_remote_copy(
            src_ref=src, dst_ref=dst, send_sem=sems.at[(0,) + slot], recv_sem=sems.at[(1,) + slot],
            device_id=where, device_id_type=MESH)
        copy.start()
        return copy

    bands, backs = [[], []], [[], []]

    def map_copy(axis, share, sender, where):
        return pltpu.make_async_remote_copy(
            src_ref=sc.msg.at[axis, share], dst_ref=sc.recv.at[axis, turn(sender, 7)],
            send_sem=sc.sem_there.at[0, axis, share], recv_sem=sc.sem_there.at[1, axis, sender],
            device_id=where, device_id_type=MESH)

    def send_maps(axis):
        pos = place[axis][0]
        sc.recv[axis, turn(pos, 7)] = sc.msg[axis, pos]
        for d in range(1, 8):
            map_copy(axis, lax.rem(pos + d, 8), pos, {"tile": peers[axis][d - 1]}).start()

    def wait_maps(axis, sent):
        pos = place[axis][0]
        for d in range(1, 8):
            peer = lax.rem(pos + d, 8)
            copy = map_copy(axis, peer if sent else 0, pos if sent else peer, {"tile": peers[axis][d - 1]})
            if sent:
                copy.wait_send()
            else:
                copy.wait_recv()

    def fold_and_send(axis):
        pos, band = place[axis]
        wait_maps(axis, False)
        for tau in range(8):
            for et in range(3):
                sc.own_f32[axis, et, tau * TS : (tau + 1) * TS, :] = sc.recv[axis, tau, 4, :, lane_block(et)].astype(jnp.float32)
        fold_lines(axis, pos, turn, sc)
        slot = turn(band, 7)
        bands[axis] = [
            push(sc.band_send.at[axis], sc.band_recv.at[axis, slot], sc.sem_band, (axis, d - 1), {"tile": peers[1 - axis][d - 1]})
            for d in range(1, 8)]
        sc.band_recv[axis, slot] = sc.band_send[axis]

    def enter_and_send(axis):
        pos, band = place[axis]
        for copy in bands[axis]:
            copy.wait_recv()
        enter_lines(axis, pos, turn(band, 7), turn, sc)
        backs[axis] = [
            push(sc.out.at[axis, turn(lax.rem(pos + d, 8), 7)], sc.back.at[axis, pos], sc.sem_back, (axis, d - 1), {"tile": peers[axis][d - 1]})
            for d in range(1, 8)]
        sc.back[axis, pos] = sc.out[axis, turn(pos, 7)]

    prepare(0, io, sc)
    local_maps(0, 0, turn, sc)
    local_maps(0, 1, turn, sc)
    pl.semaphore_wait(barrier, 22)
    send_maps(0)
    prepare(1, io, sc)
    local_maps(1, 0, turn, sc)
    local_maps(1, 1, turn, sc)
    fold_and_send(0)
    send_maps(1)
    enter_and_send(0)
    fold_and_send(1)
    enter_and_send(1)

    halves_sent = [[], []]
    own = pl.ds(pl.multiple_of(side * 8, 8), 8)
    others = pl.ds(pl.multiple_of(other * 8, 8), 8)

    def send_half(kind):
        for et in range(3):
            halves_sent[kind].append(push(sc.field.at[kind, et, :, others, :], sc.half.at[kind, et], sc.sem_half, (kind, et), partner))

    def dx_put(axis, dx):
        for j in range(16):
            sc.dx_src[j, 4 * axis : 4 * axis + 4] = dx[3 * j : 3 * j + 4]

    def dx_first():
        sc.dx_one[plane] = sc.dx_src[plane]
        return [push(sc.dx_src.at[lax.rem(plane + d, 16)], sc.dx_one.at[plane], sc.sem_dx, (0, d - 1), {"tile": in_plane[d - 1]})
                for d in range(1, 16)]

    def dx_next(arriving, phase):
        for copy in arriving:
            copy.wait_recv()
        if phase == 1:
            sc.dx_two[depth] = sum(sc.dx_one[j] for j in range(16))
            part, there = sc.dx_two.at[depth], in_depth
        else:
            sc.dx_all[plane] = sum(sc.dx_two[j] for j in range(4))
            part, there = sc.dx_all.at[plane], in_plane
        return [push(part, part, sc.sem_dx, (phase, k), {"tile": tile_to}) for k, tile_to in enumerate(there)]

    outs = []

    def merge(kind):
        for et in range(3):
            halves_sent[kind][et].wait_recv()
            total = sc.field[kind, et, :, own, :] + sc.half[kind, et]
            sc.res[kind, et, side] = total.reshape(128, 128).astype(jnp.bfloat16)
            outs.append(push(sc.res.at[kind, et, side], sc.res.at[kind, et, side], sc.sem_out, (kind, et), partner))

    def write_out(kind, ref):
        for et in range(3):
            outs[3 * kind + et].wait_recv()
            parts = [sc.res[kind, et, h].astype(jnp.float32).reshape(TS, 8, 128) for h in range(2)]
            ref[:, lane_block(et)] = jnp.concatenate(parts, axis=1).reshape(TOK, 128).astype(jnp.bfloat16)

    def both(fn, axis):
        def unit(lh, carry):
            fn(axis, lh, turn, io, sc)
            return carry

        lax.fori_loop(0, 2, unit, 0)

    def to_field(kind):
        for et in range(3):
            for i in range(TS):
                sc.field[kind, et, i] = sc.turned[kind, et, pl.ds(i, TS, stride=TS), :]

    for copy in backs[0]:
        copy.wait_recv()
    decode(0, turn(col, 7), turn, sc)
    both(scan_forward, 0)
    to_field(0)
    for copy in backs[1]:
        copy.wait_recv()
    decode(1, turn(row, 7), turn, sc)
    scan_forward(1, other, turn, io, sc)
    send_half(0)
    both(scan_backward, 0)
    dx, through = project_back(0, slice(0, TS), TS, io, sc)
    dx_put(0, dx)
    for et in range(3):
        sc.turned[1, et] = sc.turned[1, et] + through[:, lane_block(et)]
    to_field(1)
    dxs = []
    for lh, lines in ((other, others), (side, own)):
        if lh is side:
            scan_forward(1, side, turn, io, sc)
            merge(0)
        scan_backward(1, lh, turn, io, sc)
        dx, through = project_back(1, lines, 8, io, sc)
        dxs.append(dx)
        for et in range(3):
            sc.field[1, et, :, lines, :] = sc.field[1, et, :, lines, :] + through[:, lane_block(et)].reshape(TS, 8, 128)
        if lh is other:
            send_half(1)
    dx_put(1, dxs[0] + dxs[1])
    dx_sent = [dx_first()]
    dx_sent.append(dx_next(dx_sent[0], 1))
    merge(1)
    dx_sent.append(dx_next(dx_sent[1], 2))
    write_out(0, yo_ref)
    for copy in dx_sent[2]:
        copy.wait_recv()
    for j in range(15):
        for axis in range(2):
            count = min(3, 44 - 3 * j)
            dxo_ref[3 * j : 3 * j + count, axis, :] = sc.dx_all[j, 4 * axis : 4 * axis + count, :]
    write_out(1, duo_ref)
    for axis in range(2):
        wait_maps(axis, True)
    for group in bands + backs + halves_sent + [outs] + dx_sent:
        for copy in group:
            copy.wait_send()


def f32_buf(*shape):
    return pltpu.VMEM(shape, jnp.float32)


def bf16_buf(*shape):
    return pltpu.VMEM(shape, jnp.bfloat16)


def dma_sems(*shape):
    return pltpu.SemaphoreType.DMA(shape)


BUFFERS = {
    "in_x": bf16_buf(TOK, E), "in_cot": bf16_buf(TOK, E), "in_xw": bf16_buf(44, 2, E), "in_dw": bf16_buf(12, 2, E), "padded": f32_buf(128, E), "xw": bf16_buf(2, 128, E), "dw": bf16_buf(2, 128, E),
    "in_bias": f32_buf(2, E), "in_alog": f32_buf(2, NS, E), "in_skip": f32_buf(2, E), "sem_in": dma_sems(7),
    "u": f32_buf(2, TS, TS, E), "cot": f32_buf(2, TS, TS, E), "dt": f32_buf(2, TS, TS, E), "w": f32_buf(2, TS, TS, E),
    "bc": f32_buf(2, TS, TS, 4096), "rate": f32_buf(2, NS, E), "rate8": f32_buf(2, NS, 8, E), "size": f32_buf(TS, E),
    "vals": f32_buf(2, 2, 3, NS * TS, 128),
    "msg": bf16_buf(2, 8, 5, TS, E), "recv": bf16_buf(2, 8, 5, TS, E),
    "before": f32_buf(2, 3, 8 * TS, 128), "own_f32": f32_buf(2, 3, 8 * TS, 128), "total": f32_buf(2, TS, E),
    "decay": f32_buf(2, 2, 8, TS, E), "line": f32_buf(2, 6, TS, E),
    "band_send": f32_buf(2, 8, E), "band_recv": f32_buf(2, 8, 8, E),
    "ent": f32_buf(4, 3, 8 * TS, 128),
    "out": bf16_buf(2, 8, 4, TS, E), "back": bf16_buf(2, 8, 4, TS, E),
    "dbc": f32_buf(2, TS, TS, 4096), "ah": f32_buf(2, 3, 2, TS, NS, 8, 128), "ddt": f32_buf(2, TS, TS, E),
    "turned": f32_buf(2, 3, TOK, 128), "field": f32_buf(2, 3, TS, TS, 128),
    "half": f32_buf(2, 3, TS, 8, 128), "res": bf16_buf(2, 3, 2, 128, 128),
    "dx_src": f32_buf(16, 8, E), "dx_one": f32_buf(16, 8, E), "dx_two": f32_buf(4, 8, E), "dx_all": f32_buf(16, 8, E),
    "sem_there": dma_sems(2, 2, 8), "sem_band": dma_sems(2, 2, 7), "sem_back": dma_sems(2, 2, 7),
    "sem_half": dma_sems(2, 2, 3), "sem_out": dma_sems(2, 2, 3), "sem_dx": dma_sems(2, 3, 15),
}
SCRATCH = tuple(BUFFERS)
VMEM = pl.BlockSpec(memory_space=pltpu.VMEM)


def local(tiles, cotangent, xproj_w, dtproj_w, dt_bias, a_log, skip_d):
    xw = xproj_w[0].transpose(2, 0, 1)
    dw = dtproj_w[0].transpose(1, 0, 2)
    out = jax.ShapeDtypeStruct((TOK, E), jnp.bfloat16)
    yo, duo, dxo = pl.pallas_call(
        layer_kernel,
        out_shape=(out, out, jax.ShapeDtypeStruct((44, 2, E), jnp.float32)),
        in_specs=[pl.BlockSpec(memory_space=pl.ANY)] * 7,
        out_specs=(VMEM,) * 3,
        scratch_shapes=list(BUFFERS.values()),
        compiler_params=pltpu.CompilerParams(vmem_limit_bytes=56 * 2**20, collective_id=0, has_side_effects=True),
        name="layer",
    )(tiles.reshape(TOK, E), cotangent.reshape(TOK, E), xw, dw, dt_bias[0], a_log[0], skip_d[0])
    return yo.reshape(tiles.shape), duo.reshape(tiles.shape), dxo.transpose(1, 2, 0)[None]


def solution(mesh):
    by_tile = P(("scene", "tile"), None, None, None)
    by_dir = P("dir", None, None, None)
    return jax.shard_map(
        local,
        mesh=mesh,
        in_specs=(by_tile, by_tile, by_dir, by_dir, P("dir", None, None), by_dir, P("dir", None, None)),
        out_specs=(by_tile, by_tile, P(("scene", "dir"), None, None, None)),
        check_vma=False,
    )
```
